256 devices in a mesh: heads: 8 (over x, y_hi), blk: 32 (over y_lo, z, core).
Axes of the slice: x: 4, y: 4 (y_hi: 2, y_lo: 2; y = y_hi * 2 + y_lo), z: 8, core: 2. Of those that a mesh axis runs over, the one named last changes fastest.
Arguments:
- vol: bfloat16 [16384, 1024], P('blk', 'heads'), may hold values from -90 to 90
- surf: bfloat16 [4096, 1024], P('blk', 'heads'), may hold values from -40 to 40
- w_query: bfloat16 [1024, 1024], P(None, 'heads'), may hold values from -0.15625 to 0.15625
- w_key: bfloat16 [1024, 1024], P(None, 'heads'), may hold values from -0.15625 to 0.15625
- w_value: bfloat16 [1024, 1024], P(None, 'heads'), may hold values from -0.1875 to 0.1875
- grad_out: bfloat16 [16384, 1024], P('blk', 'heads'), may hold values from -24 to 24
Outputs:
- grad_vol: bfloat16 [16384, 1024], P('blk', 'heads')
- grad_surf: bfloat16 [4096, 1024], P('blk', 'heads')
- grad_wq: float32 [1024, 1024], P(None, 'heads')
- grad_wk: float32 [1024, 1024], P(None, 'heads')
- grad_wv: float32 [1024, 1024], P(None, 'heads')
The draws below stay inside these ranges and needn't reach their ends.
All inputs are finite; a program needn't handle non-finite values.
Results may differ from the reference program's by a relative error of at most 0.03.
Values may be sent and summed in bfloat16 or wider, within the bound.
A program may use at most 64 MiB of HBM per device.

```python
import jax
import jax.numpy as jnp
from jax import lax

D = 1024
HEADS = 16
HEAD_DIM = 64
NQ_DEV = 512
NQ = 16384
NK = 4096
N_BLK = 32


def shared_rows(key):
    return jnp.clip(jax.random.normal(key, (NQ, D), jnp.float32), -5.0, 5.0)


def shared_weight(key):
    inner = jax.random.fold_in(key, 100)
    return jnp.clip(jax.random.normal(inner, (D, D), jnp.float32), -5.0, 5.0) / jnp.sqrt(jnp.float32(D))


def draw_vol(key, part):
    base = shared_rows(key)
    vol = base
    return vol.astype(jnp.bfloat16)


def draw_surf(key, part):
    key = jax.random.fold_in(key, 2)
    first = jax.random.fold_in(key, 0)
    own = jnp.clip(jax.random.normal(first, (NK, D), jnp.float32), -5.0, 5.0)
    surf = own
    return surf.astype(jnp.bfloat16)


def draw_w_query(key, part):
    return shared_weight(key).astype(jnp.bfloat16)


def draw_w_key(key, part):
    own_key = jax.random.fold_in(key, 4)
    own = jnp.clip(jax.random.normal(own_key, (D, D), jnp.float32), -5.0, 5.0) / jnp.sqrt(jnp.float32(D))
    weight = own
    return weight.astype(jnp.bfloat16)


def levels(stream_key, dims, pieces, low, largest):
    level, own = 1.0, jax.random.fold_in(stream_key, 6)
    for dim, shards_of in pieces:
        draws = jnp.exp(jax.random.uniform(jax.random.fold_in(own, dim), (shards_of,), jnp.float32, low / len(pieces), largest / len(pieces)))
        level = level * jnp.repeat(draws, dims[dim] // shards_of).reshape([-1 if axis == dim else 1 for axis in range(len(dims))])
    return level


def gaussian(key, shape, spread, bound, cuts=(), held_as=jnp.bfloat16):
    gain = levels(key, shape, cuts, -0.22, 0.18) if cuts else 1.0
    entries = jax.random.normal(key, shape, jnp.float32) * spread * gain
    return jnp.minimum(jnp.maximum(entries, -bound), bound).astype(held_as)


def setup_inputs(seed: int = 0) -> dict:
    key_of = jax.random.split(jax.random.key(seed), 7)
    vol = draw_vol(jax.random.fold_in(key_of[6], 71), 0)
    surf = draw_surf(jax.random.fold_in(key_of[6], 71), 0)
    w_query = draw_w_query(jax.random.fold_in(key_of[6], 71), 0)
    w_key = draw_w_key(jax.random.fold_in(key_of[6], 71), 0)
    w_value = gaussian(key_of[4], (D, D), D ** -0.5, 0.1875, ((1, 8),))
    grad_out = gaussian(key_of[5], (NQ, D), 4.0, 24.0, ((0, 32), (1, 8)))
    return {"vol": vol, "surf": surf, "w_query": w_query, "w_key": w_key, "w_value": w_value, "grad_out": grad_out}


def head_block(query_h, key_h, value_h, grad_h):
    scale = HEAD_DIM ** -0.5
    scores = jnp.einsum('qc,kc->qk', query_h.astype(jnp.float32), key_h.astype(jnp.float32)) * scale
    top = jnp.max(scores, axis=1, keepdims=True)
    expo = jnp.exp(scores - top)
    total = jnp.sum(expo, axis=1, keepdims=True)
    probs = expo / total
    probs_b = probs.astype(jnp.bfloat16)
    output = jnp.dot(probs_b, value_h, preferred_element_type=jnp.float32)
    delta = jnp.sum(grad_h.astype(jnp.float32) * output, axis=1, keepdims=True)
    dprob = jnp.einsum('qc,kc->qk', grad_h.astype(jnp.float32), value_h.astype(jnp.float32))
    dscore = (probs * (dprob - delta) * scale).astype(jnp.bfloat16)
    dquery = jnp.dot(dscore, key_h, preferred_element_type=jnp.float32)
    dkey = jnp.einsum('qk,qc->kc', dscore.astype(jnp.float32), query_h.astype(jnp.float32))
    dvalue = jnp.einsum('qk,qc->kc', probs_b.astype(jnp.float32), grad_h.astype(jnp.float32))
    return dquery, dkey, dvalue


def reference(vol, surf, w_query, w_key, w_value, grad_out):
    query = jnp.dot(vol, w_query, preferred_element_type=jnp.float32).astype(jnp.bfloat16)
    key = jnp.dot(surf, w_key, preferred_element_type=jnp.float32).astype(jnp.bfloat16)
    value = jnp.dot(surf, w_value, preferred_element_type=jnp.float32).astype(jnp.bfloat16)
    dq_list, dk_list, dv_list = [], [], []
    for head in range(HEADS):
        cols = slice(head * HEAD_DIM, (head + 1) * HEAD_DIM)
        key_h = key[:, cols]
        value_h = value[:, cols]
        query_blocks = query[:, cols].reshape(N_BLK, NQ_DEV, HEAD_DIM)
        grad_blocks = grad_out[:, cols].reshape(N_BLK, NQ_DEV, HEAD_DIM)

        def step(carry, pair):
            dquery, dkey, dvalue = head_block(pair[0], key_h, value_h, pair[1])
            return (carry[0] + dkey, carry[1] + dvalue), dquery

        zeros = jnp.zeros((NK, HEAD_DIM), jnp.float32)
        sums, dquery = lax.scan(step, (zeros, zeros), (query_blocks, grad_blocks))
        dq_list.append(dquery.reshape(NQ, HEAD_DIM).astype(jnp.bfloat16))
        dk_list.append(sums[0].astype(jnp.bfloat16))
        dv_list.append(sums[1].astype(jnp.bfloat16))
    dquery = jnp.concatenate(dq_list, axis=1)
    dkey = jnp.concatenate(dk_list, axis=1)
    dvalue = jnp.concatenate(dv_list, axis=1)
    grad_vol = jnp.dot(dquery, w_query.T, preferred_element_type=jnp.float32).astype(jnp.bfloat16)
    grad_surf = (jnp.dot(dkey, w_key.T, preferred_element_type=jnp.float32) + jnp.dot(dvalue, w_value.T, preferred_element_type=jnp.float32)).astype(jnp.bfloat16)
    grad_wq = jnp.dot(vol.T, dquery, preferred_element_type=jnp.float32)
    grad_wk = jnp.dot(surf.T, dkey, preferred_element_type=jnp.float32)
    grad_wv = jnp.dot(surf.T, dvalue, preferred_element_type=jnp.float32)
    return grad_vol, grad_surf, grad_wq, grad_wk, grad_wv
```

```python
import jax
import jax.numpy as jnp
from jax import lax
from jax.experimental import pallas as pl
from jax.experimental.pallas import tpu as pltpu
from jax.sharding import PartitionSpec as P

HEAD_DIM = 64
MESH = pl.DeviceIdType.MESH
VMEM_LIMIT = 60 * 1024 * 1024
F32 = jnp.float32
BF16 = jnp.bfloat16
NT = (((1,), (1,)), ((), ()))
TN = (((0,), (0,)), ((), ()))

NX, NZ = 4, 8


class Place:
    def __init__(self):
        self.h = lax.axis_index("heads")
        self.b = lax.axis_index("blk")
        self.x, self.yh = self.h // 2, self.h % 2
        self.yl, self.z, self.c = self.b // 16, (self.b // 2) % NZ, self.b % 2

    def along_x(self, d):
        return (((self.x + d) % NX) * 2 + self.yh, self.b)

    def across(self, d):
        return (((self.x + d) % NX) * 2 + 1 - self.yh, self.b)

    def along_z(self, d):
        return (self.h, self.yl * 16 + ((self.z + d) % NZ) * 2 + self.c)

    def other_yl(self):
        return (self.h, (1 - self.yl) * 16 + self.z * 2 + self.c)

    def sibling(self):
        return (self.h, self.yl * 16 + self.z * 2 + 1 - self.c)

    def diagonal(self):
        return (self.h, (1 - self.yl) * 16 + self.z * 2 + 1 - self.c)


def meet(partners):
    barrier = pltpu.get_barrier_semaphore()
    for partner in partners:
        pl.semaphore_signal(barrier, inc=1, device_id=partner, device_id_type=MESH)
    pl.semaphore_wait(barrier, len(partners))


class Sender:
    def __init__(self, send_sem, recv_sem):
        self.send_sem, self.recv_sem = send_sem, recv_sem
        self.used = 0
        self.all = []

    def start(self, src, dst, device):
        copy = pltpu.make_async_remote_copy(
            src_ref=src,
            dst_ref=dst,
            send_sem=self.send_sem.at[self.used],
            recv_sem=self.recv_sem.at[self.used],
            device_id=device,
            device_id_type=MESH,
        )
        self.used += 1
        copy.start()
        self.all.append(copy)
        return copy

    def finish(self):
        for copy in self.all:
            copy.wait_send()


def whole_kernel(
    vol, surf, w_query, w_key, w_value, grad_out,
    grad_vol, grad_surf, out,
    kv, vol_full, surf_full, surf_quad, dkv_quad, x, y, m, mt, dqt, top, total, weighted,
    part, sib_in, yl_out, yl_in, ring_in, ring_out, end_in,
    vol_out, vol_in, vol_mid, vol_end, surf_out, surf_in, surf_mid, surf_end,
    q_part, q_core, q_yl, q_yl_in, z_out, z_in,
    send_sem, recv_sem,
):
    p = Place()
    h = p.h
    hp = p.x * 2 + 1 - p.yh
    rows, ctx = vol.shape[0], surf.shape[0]
    group = 4 * ctx
    pair = 2 * rows
    tiles = pair // 128
    scale = HEAD_DIM**-0.5
    heads = [p.across(d) for d in (2, 1, 3)] + [p.along_x(2), p.across(0), p.along_x(1), p.along_x(3)]
    square = [p.diagonal(), p.other_yl(), p.sibling()]
    meet(heads + square + [p.along_z(d) for d in range(1, NZ)])
    net = Sender(send_sem, recv_sem)

    surf_all = [net.start(surf, surf_full.at[h], peer) for peer in heads]
    vol_y = net.start(vol, vol_full.at[h], p.across(0))
    vol_x = [net.start(vol, vol_full.at[h], p.along_x(d)) for d in (2, 1, 3)]
    surf_full[h] = surf[...]
    vol_full[h] = vol[...]

    def place(index, block):
        turned = block.T
        col = lax.broadcasted_iota(jnp.int32, block.shape, 1)
        row = lax.broadcasted_iota(jnp.int32, turned.shape, 0)
        for head in (0, 1):
            at = index * pair + head * rows
            m[at : at + rows, index * 128 : index * 128 + 128] = jnp.where(col // HEAD_DIM == head, block, 0.0).astype(BF16)
            mt[index * 128 : index * 128 + 128, at : at + rows] = jnp.where(row // HEAD_DIM == head, turned, 0.0).astype(BF16)

    m[...] = jnp.zeros_like(m)
    mt[...] = jnp.zeros_like(mt)
    place(1, grad_out[...].astype(F32))
    top[...] = jnp.full_like(top, -jnp.inf)
    total[...] = jnp.zeros_like(total)
    weighted[...] = jnp.zeros_like(weighted)

    for copy in surf_all:
        copy.wait_recv()
    features = jnp.concatenate([surf_full[i] for i in range(8)], axis=1)
    kv[0, 0, 0, :, 0:128] = jnp.dot(features, w_key[...], preferred_element_type=F32).astype(BF16)
    kv[0, 0, 0, :, 128:256] = jnp.dot(features, w_value[...], preferred_element_type=F32).astype(BF16)

    arrivals = {}
    over_y = {}
    shared = {}

    def share(t, dz):
        shared[t, dz] = net.start(kv.at[dz, 0, t], kv.at[dz, 1, t], p.sibling())

    def hand_on(dz):
        block = kv.at[dz, 0, 0]
        if dz in (0, 7, 6, 5):
            arrivals[(dz - 1) % NZ] = net.start(block, kv.at[(dz - 1) % NZ, 0, 0], p.along_z(1))
        if dz in (0, 1, 2):
            arrivals[dz + 1] = net.start(block, kv.at[dz + 1, 0, 0], p.along_z(-1))
        over_y[dz] = net.start(block, kv.at[dz, 0, 1], p.other_yl())
        share(0, dz)

    def from_ring(*groups):
        for dz in groups:
            arrivals[dz].wait_recv()
            hand_on(dz)

    def from_y(*groups):
        for dz in groups:
            over_y[dz].wait_recv()
            share(1, dz)

    hand_on(0)
    vol_y.wait_recv()
    vol_x += [net.start(vol_full.at[hp], vol_full.at[hp], p.along_x(d)) for d in (2, 1, 3)]
    from_ring(7, 1)
    from_y(0)
    from_ring(6, 2)
    from_y(7, 1)
    from_ring(5, 3)
    for copy in vol_x:
        copy.wait_recv()
    features = jnp.concatenate([vol_full[i] for i in range(8)], axis=1)
    query = jnp.dot(features, w_query[...], preferred_element_type=F32).astype(BF16)
    place(0, query.astype(F32) * scale)

    def scan(dz):
        at = pl.ds(pl.multiple_of(dz * group, group), group)
        x[at, :] = jnp.dot(kv[dz].reshape(group, 256), mt[...], preferred_element_type=F32)
        for j in range(tiles):
            cols = slice(j * 128, j * 128 + 128)
            scores = x[at, cols].reshape(group // 8, 8, 128)
            dprob = x[at, pair + j * 128 : pair + j * 128 + 128].reshape(group // 8, 8, 128)
            before = top[:, cols]
            now = jnp.maximum(before, jnp.max(scores, axis=0))
            expo = jnp.exp(scores - now[None])
            fade = jnp.exp(before - now)
            top[:, cols] = now
            total[:, cols] = total[:, cols] * fade + jnp.sum(expo, axis=0)
            weighted[:, cols] = weighted[:, cols] * fade + jnp.sum(expo * dprob, axis=0)

    def in_turn(work, a, b):
        @pl.loop(0, 2)
        def _(i):
            work(a + i * (b - a))

    def have(*groups):
        for dz in groups:
            shared[0, dz].wait_recv()
            shared[1, dz].wait_recv()

    from_y(6, 2)
    have(0)
    scan(0)
    from_ring(4)
    from_y(5, 3)
    have(7, 1)
    in_turn(scan, 7, 1)
    from_y(4)
    quarter = p.c * 2 + p.yl
    surf_quad[0] = surf_full[pl.ds(quarter * 2, 2)]
    squares = []
    for slot, device, its in (
        (3, p.diagonal(), (1 - p.c) * 2 + 1 - p.yl),
        (2, p.other_yl(), p.c * 2 + 1 - p.yl),
        (1, p.sibling(), (1 - p.c) * 2 + p.yl),
    ):
        squares.append(net.start(surf_full.at[pl.ds(its * 2, 2)], surf_quad.at[slot], device))
    have(6, 2)
    in_turn(scan, 6, 2)
    have(5, 3)
    in_turn(scan, 5, 3)
    have(4)
    scan(4)

    best = jnp.max(top[...], axis=0, keepdims=True)
    fade = jnp.exp(top[...] - best)
    sums = jnp.sum(total[...] * fade, axis=0, keepdims=True)
    delta = jnp.sum(weighted[...] * fade, axis=0, keepdims=True) / sums
    top[...] = jnp.broadcast_to(best, top.shape)
    total[...] = jnp.broadcast_to(jnp.log(sums), total.shape)
    weighted[...] = jnp.broadcast_to(delta, weighted.shape)
    dqt[...] = jnp.zeros_like(dqt)

    def grads(dz):
        at = pl.ds(pl.multiple_of(dz * group, group), group)
        for j in range(tiles):
            cols = slice(j * 128, j * 128 + 128)
            more = slice(pair + j * 128, pair + j * 128 + 128)
            scores = x[at, cols].reshape(group // 8, 8, 128)
            dprob = x[at, more].reshape(group // 8, 8, 128)
            probs = jnp.exp((scores - top[:, cols][None]) - total[:, cols][None])
            dscore = probs * (dprob - weighted[:, cols][None])
            y[:, cols] = dscore.reshape(group, 128).astype(BF16)
            y[:, more] = probs.reshape(group, 128).astype(BF16)
        both = jnp.dot(y[...], m[...], preferred_element_type=F32)
        part[dz] = both.astype(BF16).reshape(2, 2, ctx, 256)
        keys = kv[dz].reshape(group, 256)[:, 0:128]
        dqt[...] += lax.dot_general(keys, y[:, 0:pair], TN, preferred_element_type=F32)

    sib = {}
    from_yl = {}
    ring = {}

    def to_sibling(dz):
        sib[dz] = net.start(part.at[dz, 1], sib_in.at[dz], p.sibling())

    def chip_sum(t, dz):
        return part[dz, 0, t].astype(F32) + sib_in[dz, t].astype(F32)

    def to_y(dz):
        sib[dz].wait_recv()
        yl_out[dz] = chip_sum(1, dz).astype(BF16)
        from_yl[dz] = net.start(yl_out.at[dz], yl_in.at[dz], p.other_yl())

    def both_sum(dz):
        from_yl[dz].wait_recv()
        return chip_sum(0, dz) + yl_in[dz].astype(F32)

    def send_on(dz):
        value = both_sum(dz)
        if dz not in (4, 3):
            ring[dz].wait_recv()
            value = value + ring_in[dz].astype(F32)
        ring_out[dz] = value.astype(BF16)
        way = -1 if dz >= 4 else 1
        if dz in (7, 1):
            ring[0, way] = net.start(ring_out.at[dz], end_in.at[(1 + way) // 2], p.along_z(way))
        else:
            ring[dz - way] = net.start(ring_out.at[dz], ring_in.at[dz - way], p.along_z(way))

    grads(4)
    to_sibling(4)
    grads(5)
    to_sibling(5)
    to_y(4)
    grads(3)
    to_sibling(3)
    to_y(5)
    grads(6)
    to_sibling(6)
    to_y(3)
    send_on(4)
    grads(2)
    to_sibling(2)
    to_y(6)
    send_on(3)
    grads(7)
    to_sibling(7)
    to_y(2)
    send_on(5)
    grads(1)
    to_sibling(1)
    to_y(7)
    send_on(2)
    grads(0)
    to_sibling(0)
    to_y(1)
    send_on(6)

    turned = jnp.concatenate([dqt[0:HEAD_DIM, 0:rows], dqt[HEAD_DIM:128, rows:pair]], axis=0) * scale
    dq = turned.T.astype(BF16)

    for i in range(8):
        q_part[i // 4, i // 2 % 2, (i % 2) * 128 : (i % 2) * 128 + 128, :] = lax.dot_general(
            vol_full[i], dq, TN, preferred_element_type=F32
        ).astype(BF16)
    q_sib = net.start(q_part.at[1 - p.c], q_core, p.sibling())
    to_y(0)
    send_on(1)
    send_on(7)
    for i in range(NX):
        vol_out[i] = lax.dot_general(dq, w_query[i * 256 : i * 256 + 256, :], NT, preferred_element_type=F32).astype(BF16)
    vol_x = [net.start(vol_out.at[(p.x + d) % NX], vol_in.at[d - 1], p.along_x(d)) for d in (2, 1, 3)]
    q_sib.wait_recv()
    q_yl[...] = (q_part[p.c].astype(F32) + q_core[...].astype(F32)).astype(BF16)
    q_copy = net.start(q_yl.at[1 - p.yl], q_yl_in, p.other_yl())

    own = both_sum(0)
    ring[0, 1].wait_recv()
    own = own + end_in[1].astype(F32)
    ring[0, -1].wait_recv()
    dkv_quad[0] = (own + end_in[0].astype(F32)).astype(BF16)
    dkv_copies = [net.start(dkv_quad.at[0], dkv_quad.at[3 - i], square[i]) for i in range(3)]
    dkv = dkv_quad[0]
    for i in range(NX):
        weights = jnp.concatenate([w_key[i * 256 : i * 256 + 256, :], w_value[i * 256 : i * 256 + 256, :]], axis=1)
        surf_out[i] = lax.dot_general(dkv, weights, NT, preferred_element_type=F32).astype(BF16)
    surf_x = [net.start(surf_out.at[(p.x + d) % NX], surf_in.at[d - 1], p.along_x(d)) for d in (2, 1, 3)]
    q_copy.wait_recv()
    z_out[:, :, 256:384] = (q_yl[p.yl].astype(F32) + q_yl_in[...].astype(F32)).reshape(NZ, 32, 128).astype(BF16)

    for copy in squares + dkv_copies:
        copy.wait_recv()
    dkv = dkv_quad[...].reshape(4 * ctx, 256)
    for i in range(2):
        points = jnp.concatenate([surf_quad[j, i] for j in range(4)], axis=0)
        block = lax.dot_general(points, dkv, TN, preferred_element_type=F32).astype(BF16)
        z_out[i * 4 : i * 4 + 4, :, 0:256] = block.reshape(4, 32, 256)

    far_first = (4, 3, 5, 2, 6, 1, 7)
    scattered = [net.start(z_out.at[(p.z + d) % NZ], z_in.at[d - 1], p.along_z(d)) for d in far_first]
    for copy in scattered:
        copy.wait_recv()
    sums = z_out[p.z].astype(F32)
    for i in range(NZ - 1):
        sums = sums + z_in[i].astype(F32)
    out[quarter, p.z] = sums.astype(BF16)

    def forward(dz):
        block = out.at[quarter, (p.z + dz) % NZ]
        return net.start(block, block, p.other_yl())

    mine = out.at[quarter, p.z]
    gathered = {d: net.start(mine, mine, p.along_z(d)) for d in far_first}
    forwarded = [forward(0)]

    def sum_x(copies, out, arrived, mid):
        for copy in copies:
            copy.wait_recv()
        sums = out[p.x].astype(F32)
        for i in range(NX - 1):
            sums = sums + arrived[i].astype(F32)
        mid[0] = sums[:, 0:128].astype(BF16)
        mid[1] = sums[:, 128:256].astype(BF16)

    sum_x(vol_x, vol_out, vol_in, vol_mid)
    vol_copy = net.start(vol_mid.at[1 - p.yh], vol_end, p.across(0))
    sum_x(surf_x, surf_out, surf_in, surf_mid)
    surf_copy = net.start(surf_mid.at[1 - p.yh], surf_end, p.across(0))
    for dz in (1, 7, 2, 6, 3, 5, 4):
        gathered[NZ - dz].wait_recv()
        forwarded.append(forward(dz))
    to_core = [net.start(out.at[quarter], out.at[quarter], p.sibling())]
    vol_copy.wait_recv()
    grad_vol[...] = (vol_mid[p.yh].astype(F32) + vol_end[...].astype(F32)).astype(BF16)
    surf_copy.wait_recv()
    grad_surf[...] = (surf_mid[p.yh].astype(F32) + surf_end[...].astype(F32)).astype(BF16)
    for copy in forwarded:
        copy.wait_recv()
    theirs = out.at[p.c * 2 + 1 - p.yl]
    to_core.append(net.start(theirs, theirs, p.sibling()))
    for copy in to_core:
        copy.wait_recv()
    net.finish()


def finish_kernel(vol_in, surf_in, w_in, grad_vol, grad_surf, grad_wq, grad_wk, grad_wv):
    grad_vol[...] = vol_in[...]
    grad_surf[...] = surf_in[...]
    grad_wk[...] = w_in[:, 0:128].astype(F32)
    grad_wv[...] = w_in[:, 128:256].astype(F32)
    grad_wq[...] = w_in[:, 256:384].astype(F32)


def in_vmem(count):
    return [pl.BlockSpec(memory_space=pltpu.VMEM)] * count


def struct(*shape):
    return jax.ShapeDtypeStruct(shape, BF16)


def on_device(vol, surf, w_query, w_key, w_value, grad_out):
    rows, ctx = vol.shape[0], surf.shape[0]
    pair = 2 * rows
    group = 4 * ctx

    def over_x(n):
        return [
            pltpu.VMEM((NX, n, 256), BF16), pltpu.VMEM((NX - 1, n, 256), BF16),
            pltpu.VMEM((2, n, 128), BF16), pltpu.VMEM((n, 128), BF16),
        ]

    grad_vol, grad_surf, out = pl.pallas_call(
        whole_kernel,
        out_shape=[struct(rows, 128), struct(ctx, 128), struct(4, NZ, 32, 384)],
        in_specs=in_vmem(6),
        out_specs=in_vmem(3),
        scratch_shapes=[
            pltpu.VMEM((NZ, 2, 2, ctx, 256), BF16),
            pltpu.VMEM((8, rows, 128), BF16),
            pltpu.VMEM((8, ctx, 128), BF16),
            pltpu.VMEM((4, 2, ctx, 128), BF16),
            pltpu.VMEM((4, ctx, 256), BF16),
            pltpu.VMEM((NZ * group, 2 * pair), F32),
            pltpu.VMEM((group, 2 * pair), BF16),
            pltpu.VMEM((2 * pair, 256), BF16),
            pltpu.VMEM((256, 2 * pair), BF16),
            pltpu.VMEM((128, pair), F32),
            pltpu.VMEM((8, pair), F32),
            pltpu.VMEM((8, pair), F32),
            pltpu.VMEM((8, pair), F32),
            pltpu.VMEM((NZ, 2, 2, ctx, 256), BF16),
            pltpu.VMEM((NZ, 2, ctx, 256), BF16),
            pltpu.VMEM((NZ, ctx, 256), BF16),
            pltpu.VMEM((NZ, ctx, 256), BF16),
            pltpu.VMEM((NZ, ctx, 256), BF16),
            pltpu.VMEM((NZ, ctx, 256), BF16),
            pltpu.VMEM((2, ctx, 256), BF16),
        ]
        + over_x(rows) + over_x(ctx)
        + [
            pltpu.VMEM((2, 2, 256, 128), BF16),
            pltpu.VMEM((2, 256, 128), BF16),
            pltpu.VMEM((2, 256, 128), BF16),
            pltpu.VMEM((256, 128), BF16),
            pltpu.VMEM((NZ, 32, 384), BF16),
            pltpu.VMEM((NZ - 1, 32, 384), BF16),
        ]
        + [pltpu.SemaphoreType.DMA((120,)), pltpu.SemaphoreType.DMA((120,))],
        compiler_params=pltpu.CompilerParams(collective_id=0, has_side_effects=True, vmem_limit_bytes=VMEM_LIMIT),
    )(vol, surf, w_query, w_key, w_value, grad_out)

    wide = jax.ShapeDtypeStruct((1024, 128), F32)
    return pl.pallas_call(
        finish_kernel,
        out_shape=[struct(rows, 128), struct(ctx, 128), wide, wide, wide],
        in_specs=in_vmem(3),
        out_specs=in_vmem(5),
    )(grad_vol, grad_surf, out.reshape(1024, 384))


def solution(mesh):
    in_specs = (
        P("blk", "heads"),
        P("blk", "heads"),
        P(None, "heads"),
        P(None, "heads"),
        P(None, "heads"),
        P("blk", "heads"),
    )
    out_specs = (
        P("blk", "heads"),
        P("blk", "heads"),
        P(None, "heads"),
        P(None, "heads"),
        P(None, "heads"),
    )
    return jax.shard_map(
        on_device, mesh=mesh, in_specs=in_specs, out_specs=out_specs, check_vma=False
    )
```

```python
import jax
import jax.numpy as jnp
from jax import lax
from jax.experimental import pallas as pl
from jax.experimental.pallas import tpu as pltpu
from jax.sharding import PartitionSpec as P

HEAD_DIM = 64
MESH = pl.DeviceIdType.MESH
VMEM_LIMIT = 60 * 1024 * 1024
F32 = jnp.float32
BF16 = jnp.bfloat16
NT = (((1,), (1,)), ((), ()))
TN = (((0,), (0,)), ((), ()))

NX, NZ = 4, 8


class Place:
    def __init__(self):
        self.h = lax.axis_index("heads")
        self.b = lax.axis_index("blk")
        self.x, self.yh = self.h // 2, self.h % 2
        self.yl, self.z, self.c = self.b // 16, (self.b // 2) % NZ, self.b % 2

    def along_x(self, d):
        return (((self.x + d) % NX) * 2 + self.yh, self.b)

    def across(self, d):
        return (((self.x + d) % NX) * 2 + 1 - self.yh, self.b)

    def along_z(self, d):
        return (self.h, self.yl * 16 + ((self.z + d) % NZ) * 2 + self.c)

    def other_yl(self):
        return (self.h, (1 - self.yl) * 16 + self.z * 2 + self.c)

    def sibling(self):
        return (self.h, self.yl * 16 + self.z * 2 + 1 - self.c)

    def diagonal(self):
        return (self.h, (1 - self.yl) * 16 + self.z * 2 + 1 - self.c)


def meet(partners):
    barrier = pltpu.get_barrier_semaphore()
    for partner in partners:
        pl.semaphore_signal(barrier, inc=1, device_id=partner, device_id_type=MESH)
    pl.semaphore_wait(barrier, len(partners))


class Sender:
    def __init__(self, send_sem, recv_sem):
        self.send_sem, self.recv_sem = send_sem, recv_sem
        self.used = 0
        self.all = []

    def start(self, src, dst, device):
        copy = pltpu.make_async_remote_copy(
            src_ref=src,
            dst_ref=dst,
            send_sem=self.send_sem.at[self.used],
            recv_sem=self.recv_sem.at[self.used],
            device_id=device,
            device_id_type=MESH,
        )
        self.used += 1
        copy.start()
        self.all.append(copy)
        return copy

    def finish(self):
        for copy in self.all:
            copy.wait_send()


def whole_kernel(
    vol, surf, w_query, w_key, w_value, grad_out,
    grad_vol, grad_surf, out,
    kv, vol_full, surf_full, w_far, query_out, query_in, surf_quad, dkv_quad, x, y, m, mt, dqt, top, total, weighted,
    part, sib_in, yl_out, yl_in, ring_out, ring_in,
    vol_out, vol_in, vol_mid, vol_end, surf_out, surf_in, surf_mid, surf_end,
    q_part, q_core, q_yl, q_yl_in, z_out, z_in,
    send_sem, recv_sem,
):
    p = Place()
    h = p.h
    hp = p.x * 2 + 1 - p.yh
    rows, ctx = vol.shape[0], surf.shape[0]
    group = 4 * ctx
    pair = 2 * rows
    tiles = pair // 128
    scale = HEAD_DIM**-0.5
    heads = [p.across(d) for d in (2, 1, 3)] + [p.along_x(2), p.across(0), p.along_x(1), p.along_x(3)]
    square = [p.diagonal(), p.other_yl(), p.sibling()]
    meet(heads + square + [p.along_z(d) for d in range(1, NZ)])
    net = Sender(send_sem, recv_sem)

    surf_all = [net.start(surf, surf_full.at[h], peer) for peer in heads]
    vol_x = [net.start(vol, vol_full.at[h], p.along_x(d)) for d in (2, 1, 3)]
    far = []
    for i in range(NX):
        rows_far = pl.ds(pl.multiple_of((i * 2 + 1 - p.yh) * 128, 128), 128)
        far.append(net.start(w_query.at[rows_far], w_far.at[pl.ds(i * 128, 128)], p.across(0)))
    surf_full[h] = surf[...]
    vol_full[h] = vol[...]

    def place(index, block):
        turned = block.T
        col = lax.broadcasted_iota(jnp.int32, block.shape, 1)
        row = lax.broadcasted_iota(jnp.int32, turned.shape, 0)
        for head in (0, 1):
            at = index * pair + head * rows
            m[at : at + rows, index * 128 : index * 128 + 128] = jnp.where(col // HEAD_DIM == head, block, 0.0).astype(BF16)
            mt[index * 128 : index * 128 + 128, at : at + rows] = jnp.where(row // HEAD_DIM == head, turned, 0.0).astype(BF16)

    m[...] = jnp.zeros_like(m)
    mt[...] = jnp.zeros_like(mt)
    place(1, grad_out[...].astype(F32))
    top[...] = jnp.full_like(top, -jnp.inf)
    total[...] = jnp.zeros_like(total)
    weighted[...] = jnp.zeros_like(weighted)

    for copy in surf_all:
        copy.wait_recv()
    features = jnp.concatenate([surf_full[i] for i in range(8)], axis=1)
    kv[0, 0, 0, :, 0:128] = jnp.dot(features, w_key[...], preferred_element_type=F32).astype(BF16)
    kv[0, 0, 0, :, 128:256] = jnp.dot(features, w_value[...], preferred_element_type=F32).astype(BF16)

    arrivals = {}
    over_y = {}
    shared = {}

    def share(t, dz):
        shared[t, dz] = net.start(kv.at[dz, 0, t], kv.at[dz, 1, t], p.sibling())

    def hand_on(dz):
        over_y[dz] = net.start(kv.at[dz, 0, 0], kv.at[dz, 0, 1], p.other_yl())
        share(0, dz)

    def from_z(*groups):
        for dz in groups:
            arrivals[dz].wait_recv()
            hand_on(dz)

    def from_y(*groups):
        for dz in groups:
            over_y[dz].wait_recv()
            share(1, dz)

    far_first = (4, 3, 5, 2, 6, 1, 7)
    for d in far_first:
        arrivals[NZ - d] = net.start(kv.at[0, 0, 0], kv.at[NZ - d, 0, 0], p.along_z(d))
    hand_on(0)
    from_z(7, 1)
    from_y(0)

    for copy in vol_x + far:
        copy.wait_recv()
    features = jnp.concatenate([vol_full[i * 2 + p.yh] for i in range(NX)], axis=1)
    query_out[...] = jnp.dot(features, w_far[...], preferred_element_type=F32).astype(BF16)
    query_copy = net.start(query_out, query_in, p.across(0))
    vol_y = net.start(vol, vol_full.at[h], p.across(0))
    near = [w_query[pl.ds(pl.multiple_of((i * 2 + p.yh) * 128, 128), 128), :] for i in range(NX)]
    query = jnp.dot(features, jnp.concatenate(near, axis=0), preferred_element_type=F32)
    from_z(6, 2)
    from_y(7, 1)
    query_copy.wait_recv()
    query = (query + query_in[...].astype(F32)).astype(BF16)
    place(0, query.astype(F32) * scale)

    def scan(dz):
        at = pl.ds(pl.multiple_of(dz * group, group), group)
        x[at, :] = jnp.dot(kv[dz].reshape(group, 256), mt[...], preferred_element_type=F32)
        for j in range(tiles):
            cols = slice(j * 128, j * 128 + 128)
            scores = x[at, cols].reshape(group // 8, 8, 128)
            dprob = x[at, pair + j * 128 : pair + j * 128 + 128].reshape(group // 8, 8, 128)
            before = top[:, cols]
            now = jnp.maximum(before, jnp.max(scores, axis=0))
            expo = jnp.exp(scores - now[None])
            fade = jnp.exp(before - now)
            top[:, cols] = now
            total[:, cols] = total[:, cols] * fade + jnp.sum(expo, axis=0)
            weighted[:, cols] = weighted[:, cols] * fade + jnp.sum(expo * dprob, axis=0)

    def have(*groups):
        for dz in groups:
            shared[0, dz].wait_recv()
            shared[1, dz].wait_recv()

    from_z(5, 3)
    from_y(6, 2)
    have(0)
    scan(0)
    from_z(4)
    from_y(5, 3)
    vol_y.wait_recv()
    vol_x = [net.start(vol_full.at[hp], vol_full.at[hp], p.along_x(d)) for d in (2, 1, 3)]
    have(7, 1)
    scan(7)
    scan(1)
    from_y(4)
    quarter = p.c * 2 + p.yl
    surf_quad[0] = surf_full[pl.ds(quarter * 2, 2)]
    squares = []
    for slot, device, its in (
        (3, p.diagonal(), (1 - p.c) * 2 + 1 - p.yl),
        (2, p.other_yl(), p.c * 2 + 1 - p.yl),
        (1, p.sibling(), (1 - p.c) * 2 + p.yl),
    ):
        squares.append(net.start(surf_full.at[pl.ds(its * 2, 2)], surf_quad.at[slot], device))
    have(6, 2)
    scan(6)
    scan(2)
    have(5, 3)
    scan(5)
    scan(3)
    have(4)
    scan(4)

    best = jnp.max(top[...], axis=0, keepdims=True)
    fade = jnp.exp(top[...] - best)
    sums = jnp.sum(total[...] * fade, axis=0, keepdims=True)
    delta = jnp.sum(weighted[...] * fade, axis=0, keepdims=True) / sums
    top[...] = jnp.broadcast_to(best, top.shape)
    total[...] = jnp.broadcast_to(jnp.log(sums), total.shape)
    weighted[...] = jnp.broadcast_to(delta, weighted.shape)
    dqt[...] = jnp.zeros_like(dqt)

    def grads(dz):
        at = pl.ds(pl.multiple_of(dz * group, group), group)
        for j in range(tiles):
            cols = slice(j * 128, j * 128 + 128)
            more = slice(pair + j * 128, pair + j * 128 + 128)
            scores = x[at, cols].reshape(group // 8, 8, 128)
            dprob = x[at, more].reshape(group // 8, 8, 128)
            probs = jnp.exp((scores - top[:, cols][None]) - total[:, cols][None])
            dscore = probs * (dprob - weighted[:, cols][None])
            y[:, cols] = dscore.reshape(group, 128).astype(BF16)
            y[:, more] = probs.reshape(group, 128).astype(BF16)
        both = jnp.dot(y[...], m[...], preferred_element_type=F32)
        part[dz] = both.astype(BF16).reshape(2, 2, ctx, 256)
        keys = kv[dz].reshape(group, 256)[:, 0:128]
        dqt[...] += lax.dot_general(keys, y[:, 0:pair], TN, preferred_element_type=F32)

    sib = {}
    from_yl = {}
    from_peer = []

    def to_sibling(dz):
        sib[dz] = net.start(part.at[dz, 1], sib_in.at[dz], p.sibling())

    def chip_sum(t, dz):
        return part[dz, 0, t].astype(F32) + sib_in[dz, t].astype(F32)

    def to_y(dz):
        sib[dz].wait_recv()
        yl_out[dz] = chip_sum(1, dz).astype(BF16)
        from_yl[dz] = net.start(yl_out.at[dz], yl_in.at[dz], p.other_yl())

    def both_sum(dz):
        from_yl[dz].wait_recv()
        return chip_sum(0, dz) + yl_in[dz].astype(F32)

    def to_peer(dz):
        ring_out[dz] = both_sum(dz).astype(BF16)
        from_peer.append(net.start(ring_out.at[dz], ring_in.at[dz - 1], p.along_z(dz)))

    order = (4, 5, 3, 6, 2, 7, 1, 0)
    for i, dz in enumerate(order):
        grads(dz)
        to_sibling(dz)
        if i >= 2:
            to_y(order[i - 2])
        if i >= 5:
            to_peer(order[i - 5])

    turned = jnp.concatenate([dqt[0:HEAD_DIM, 0:rows], dqt[HEAD_DIM:128, rows:pair]], axis=0) * scale
    dq = turned.T.astype(BF16)

    for copy in vol_x:
        copy.wait_recv()
    for i in range(8):
        q_part[i // 4, i // 2 % 2, (i % 2) * 128 : (i % 2) * 128 + 128, :] = lax.dot_general(
            vol_full[i], dq, TN, preferred_element_type=F32
        ).astype(BF16)
    q_sib = net.start(q_part.at[1 - p.c], q_core, p.sibling())
    to_y(1)
    to_peer(6)
    to_y(0)
    to_peer(2)
    for i in range(NX):
        vol_out[i] = lax.dot_general(dq, w_query[i * 256 : i * 256 + 256, :], NT, preferred_element_type=F32).astype(BF16)
    vol_x = [net.start(vol_out.at[(p.x + d) % NX], vol_in.at[d - 1], p.along_x(d)) for d in (2, 1, 3)]
    to_peer(7)
    to_peer(1)
    q_sib.wait_recv()
    q_yl[...] = (q_part[p.c].astype(F32) + q_core[...].astype(F32)).astype(BF16)
    q_copy = net.start(q_yl.at[1 - p.yl], q_yl_in, p.other_yl())

    own = both_sum(0)
    for copy in from_peer:
        copy.wait_recv()
    for i in range(NZ - 1):
        own = own + ring_in[i].astype(F32)
    dkv_quad[0] = own.astype(BF16)
    dkv_copies = [net.start(dkv_quad.at[0], dkv_quad.at[3 - i], square[i]) for i in range(3)]
    dkv = dkv_quad[0]
    for i in range(NX):
        weights = jnp.concatenate([w_key[i * 256 : i * 256 + 256, :], w_value[i * 256 : i * 256 + 256, :]], axis=1)
        surf_out[i] = lax.dot_general(dkv, weights, NT, preferred_element_type=F32).astype(BF16)
    surf_x = [net.start(surf_out.at[(p.x + d) % NX], surf_in.at[d - 1], p.along_x(d)) for d in (2, 1, 3)]
    q_copy.wait_recv()
    z_out[:, :, 256:384] = (q_yl[p.yl].astype(F32) + q_yl_in[...].astype(F32)).reshape(NZ, 32, 128).astype(BF16)

    for copy in squares + dkv_copies:
        copy.wait_recv()
    dkv = dkv_quad[...].reshape(4 * ctx, 256)
    for i in range(2):
        points = jnp.concatenate([surf_quad[j, i] for j in range(4)], axis=0)
        block = lax.dot_general(points, dkv, TN, preferred_element_type=F32).astype(BF16)
        z_out[i * 4 : i * 4 + 4, :, 0:256] = block.reshape(4, 32, 256)

    scattered = [net.start(z_out.at[(p.z + d) % NZ], z_in.at[d - 1], p.along_z(d)) for d in far_first]
    for copy in scattered:
        copy.wait_recv()
    sums = z_out[p.z].astype(F32)
    for i in range(NZ - 1):
        sums = sums + z_in[i].astype(F32)
    out[quarter, p.z] = sums.astype(BF16)

    def forward(dz):
        block = out.at[quarter, (p.z + dz) % NZ]
        return net.start(block, block, p.other_yl())

    mine = out.at[quarter, p.z]
    gathered = {d: net.start(mine, mine, p.along_z(d)) for d in far_first}
    forwarded = [forward(0)]

    def sum_x(copies, out, arrived, mid):
        for copy in copies:
            copy.wait_recv()
        sums = out[p.x].astype(F32)
        for i in range(NX - 1):
            sums = sums + arrived[i].astype(F32)
        mid[0] = sums[:, 0:128].astype(BF16)
        mid[1] = sums[:, 128:256].astype(BF16)

    sum_x(vol_x, vol_out, vol_in, vol_mid)
    vol_copy = net.start(vol_mid.at[1 - p.yh], vol_end, p.across(0))
    sum_x(surf_x, surf_out, surf_in, surf_mid)
    surf_copy = net.start(surf_mid.at[1 - p.yh], surf_end, p.across(0))
    for dz in (1, 7, 2, 6, 3, 5, 4):
        gathered[NZ - dz].wait_recv()
        forwarded.append(forward(dz))
    to_core = [net.start(out.at[quarter], out.at[quarter], p.sibling())]
    vol_copy.wait_recv()
    grad_vol[...] = (vol_mid[p.yh].astype(F32) + vol_end[...].astype(F32)).astype(BF16)
    surf_copy.wait_recv()
    grad_surf[...] = (surf_mid[p.yh].astype(F32) + surf_end[...].astype(F32)).astype(BF16)
    for copy in forwarded:
        copy.wait_recv()
    theirs = out.at[p.c * 2 + 1 - p.yl]
    to_core.append(net.start(theirs, theirs, p.sibling()))
    for copy in to_core:
        copy.wait_recv()
    net.finish()


def finish_kernel(vol_in, surf_in, w_in, grad_vol, grad_surf, grad_wq, grad_wk, grad_wv):
    grad_vol[...] = vol_in[...]
    grad_surf[...] = surf_in[...]
    grad_wk[...] = w_in[:, 0:128].astype(F32)
    grad_wv[...] = w_in[:, 128:256].astype(F32)
    grad_wq[...] = w_in[:, 256:384].astype(F32)


def in_vmem(count):
    return [pl.BlockSpec(memory_space=pltpu.VMEM)] * count


def struct(*shape):
    return jax.ShapeDtypeStruct(shape, BF16)


def on_device(vol, surf, w_query, w_key, w_value, grad_out):
    rows, ctx = vol.shape[0], surf.shape[0]
    pair = 2 * rows
    group = 4 * ctx

    def over_x(n):
        return [
            pltpu.VMEM((NX, n, 256), BF16), pltpu.VMEM((NX - 1, n, 256), BF16),
            pltpu.VMEM((2, n, 128), BF16), pltpu.VMEM((n, 128), BF16),
        ]

    grad_vol, grad_surf, out = pl.pallas_call(
        whole_kernel,
        out_shape=[struct(rows, 128), struct(ctx, 128), struct(4, NZ, 32, 384)],
        in_specs=in_vmem(6),
        out_specs=in_vmem(3),
        scratch_shapes=[
            pltpu.VMEM((NZ, 2, 2, ctx, 256), BF16),
            pltpu.VMEM((8, rows, 128), BF16),
            pltpu.VMEM((8, ctx, 128), BF16),
            pltpu.VMEM((512, 128), BF16),
            pltpu.VMEM((rows, 128), BF16),
            pltpu.VMEM((rows, 128), BF16),
            pltpu.VMEM((4, 2, ctx, 128), BF16),
            pltpu.VMEM((4, ctx, 256), BF16),
            pltpu.VMEM((NZ * group, 2 * pair), F32),
            pltpu.VMEM((group, 2 * pair), BF16),
            pltpu.VMEM((2 * pair, 256), BF16),
            pltpu.VMEM((256, 2 * pair), BF16),
            pltpu.VMEM((128, pair), F32),
            pltpu.VMEM((8, pair), F32),
            pltpu.VMEM((8, pair), F32),
            pltpu.VMEM((8, pair), F32),
            pltpu.VMEM((NZ, 2, 2, ctx, 256), BF16),
            pltpu.VMEM((NZ, 2, ctx, 256), BF16),
            pltpu.VMEM((NZ, ctx, 256), BF16),
            pltpu.VMEM((NZ, ctx, 256), BF16),
            pltpu.VMEM((NZ, ctx, 256), BF16),
            pltpu.VMEM((NZ - 1, ctx, 256), BF16),
        ]
        + over_x(rows) + over_x(ctx)
        + [
            pltpu.VMEM((2, 2, 256, 128), BF16),
            pltpu.VMEM((2, 256, 128), BF16),
            pltpu.VMEM((2, 256, 128), BF16),
            pltpu.VMEM((256, 128), BF16),
            pltpu.VMEM((NZ, 32, 384), BF16),
            pltpu.VMEM((NZ - 1, 32, 384), BF16),
        ]
        + [pltpu.SemaphoreType.DMA((120,)), pltpu.SemaphoreType.DMA((120,))],
        compiler_params=pltpu.CompilerParams(collective_id=0, has_side_effects=True, vmem_limit_bytes=VMEM_LIMIT),
    )(vol, surf, w_query, w_key, w_value, grad_out)

    wide = jax.ShapeDtypeStruct((1024, 128), F32)
    return pl.pallas_call(
        finish_kernel,
        out_shape=[struct(rows, 128), struct(ctx, 128), wide, wide, wide],
        in_specs=in_vmem(3),
        out_specs=in_vmem(5),
    )(grad_vol, grad_surf, out.reshape(1024, 384))


def solution(mesh):
    in_specs = (
        P("blk", "heads"),
        P("blk", "heads"),
        P(None, "heads"),
        P(None, "heads"),
        P(None, "heads"),
        P("blk", "heads"),
    )
    out_specs = (
        P("blk", "heads"),
        P("blk", "heads"),
        P(None, "heads"),
        P(None, "heads"),
        P(None, "heads"),
    )
    return jax.shard_map(
        on_device, mesh=mesh, in_specs=in_specs, out_specs=out_specs, check_vma=False
    )
```

```python
import jax
import jax.numpy as jnp
from jax import lax
from jax.experimental import pallas as pl
from jax.experimental.pallas import tpu as pltpu
from jax.sharding import PartitionSpec as P

HEAD_DIM = 64
MESH = pl.DeviceIdType.MESH
VMEM_LIMIT = 60 * 1024 * 1024
F32 = jnp.float32
BF16 = jnp.bfloat16
NT = (((1,), (1,)), ((), ()))
TN = (((0,), (0,)), ((), ()))

NX, NZ = 4, 8


class Place:
    def __init__(self):
        self.h = lax.axis_index("heads")
        self.b = lax.axis_index("blk")
        self.x, self.yh = self.h // 2, self.h % 2
        self.yl, self.z, self.c = self.b // 16, (self.b // 2) % NZ, self.b % 2

    def along_x(self, d):
        return (((self.x + d) % NX) * 2 + self.yh, self.b)

    def across(self, d):
        return (((self.x + d) % NX) * 2 + 1 - self.yh, self.b)

    def along_z(self, d):
        return (self.h, self.yl * 16 + ((self.z + d) % NZ) * 2 + self.c)

    def other_yl(self):
        return (self.h, (1 - self.yl) * 16 + self.z * 2 + self.c)

    def sibling(self):
        return (self.h, self.yl * 16 + self.z * 2 + 1 - self.c)

    def diagonal(self):
        return (self.h, (1 - self.yl) * 16 + self.z * 2 + 1 - self.c)


def meet(partners):
    barrier = pltpu.get_barrier_semaphore()
    for partner in partners:
        pl.semaphore_signal(barrier, inc=1, device_id=partner, device_id_type=MESH)
    pl.semaphore_wait(barrier, len(partners))


class Sender:
    def __init__(self, send_sem, recv_sem):
        self.send_sem, self.recv_sem = send_sem, recv_sem
        self.used = 0
        self.all = []

    def start(self, src, dst, device):
        copy = pltpu.make_async_remote_copy(
            src_ref=src,
            dst_ref=dst,
            send_sem=self.send_sem.at[self.used],
            recv_sem=self.recv_sem.at[self.used],
            device_id=device,
            device_id_type=MESH,
        )
        self.used += 1
        copy.start()
        self.all.append(copy)
        return copy

    def finish(self):
        for copy in self.all:
            copy.wait_send()


def whole_kernel(
    vol, surf, w_query, w_key, w_value, grad_out,
    grad_vol, grad_surf, out,
    kv, vol_full, surf_full, w_far, query_out, query_in, surf_quad, dkv_quad, x, y, m, mt, dqt, top, total, weighted,
    part, sib_in, yl_out, yl_in, z_sums, step_in, half_in, end_in,
    vol_out, vol_in, vol_mid, vol_end, surf_out, surf_in, surf_mid, surf_end,
    q_part, q_core, q_yl, q_yl_in, z_out, z_in,
    send_sem, recv_sem,
):
    p = Place()
    h = p.h
    hp = p.x * 2 + 1 - p.yh
    rows, ctx = vol.shape[0], surf.shape[0]
    group = 4 * ctx
    pair = 2 * rows
    tiles = pair // 128
    scale = HEAD_DIM**-0.5
    heads = [p.across(d) for d in (2, 1, 3)] + [p.along_x(2), p.across(0), p.along_x(1), p.along_x(3)]
    square = [p.diagonal(), p.other_yl(), p.sibling()]
    meet(heads + square + [p.along_z(d) for d in range(1, NZ)])
    net = Sender(send_sem, recv_sem)

    surf_all = [net.start(surf, surf_full.at[h], peer) for peer in heads]
    vol_x = [net.start(vol, vol_full.at[h], p.along_x(d)) for d in (2, 1, 3)]
    far = []
    for i in range(NX):
        rows_far = pl.ds(pl.multiple_of((i * 2 + 1 - p.yh) * 128, 128), 128)
        far.append(net.start(w_query.at[rows_far], w_far.at[pl.ds(i * 128, 128)], p.across(0)))
    surf_full[h] = surf[...]
    vol_full[h] = vol[...]

    def place(index, block):
        turned = block.T
        col = lax.broadcasted_iota(jnp.int32, block.shape, 1)
        row = lax.broadcasted_iota(jnp.int32, turned.shape, 0)
        for head in (0, 1):
            at = index * pair + head * rows
            m[at : at + rows, index * 128 : index * 128 + 128] = jnp.where(col // HEAD_DIM == head, block, 0.0).astype(BF16)
            mt[index * 128 : index * 128 + 128, at : at + rows] = jnp.where(row // HEAD_DIM == head, turned, 0.0).astype(BF16)

    m[...] = jnp.zeros_like(m)
    mt[...] = jnp.zeros_like(mt)
    place(1, grad_out[...].astype(F32))
    top[...] = jnp.full_like(top, -jnp.inf)
    total[...] = jnp.zeros_like(total)
    weighted[...] = jnp.zeros_like(weighted)

    for copy in surf_all:
        copy.wait_recv()
    features = jnp.concatenate([surf_full[i] for i in range(8)], axis=1)
    kv[0, 0, 0, :, 0:128] = jnp.dot(features, w_key[...], preferred_element_type=F32).astype(BF16)
    kv[0, 0, 0, :, 128:256] = jnp.dot(features, w_value[...], preferred_element_type=F32).astype(BF16)

    arrivals = {}
    over_y = {}
    shared = {}
    mid = ctx // 2
    upper, lower = slice(0, mid), slice(mid, ctx)

    def share(t, dz):
        shared[t, dz] = net.start(kv.at[dz, 0, t], kv.at[dz, 1, t], p.sibling())

    def along(dz, d):
        to = (dz - d) % NZ
        arrivals[to] = [net.start(kv.at[dz, 0, 0], kv.at[to, 0, 0], p.along_z(d))]

    def hand_on(dz):
        over_y[dz] = net.start(kv.at[dz, 0, 0], kv.at[dz, 0, 1], p.other_yl())
        share(0, dz)

    def from_z(*groups):
        for dz in groups:
            for copy in arrivals[dz]:
                copy.wait_recv()
            if dz == 6:
                along(6, 1)
                from_below = net.start(kv.at[6, 0, 0, upper], kv.at[4, 0, 0, upper], p.along_z(2))
            if dz == 2:
                along(2, -1)
                from_above = net.start(kv.at[2, 0, 0, lower], kv.at[4, 0, 0, lower], p.along_z(-2))
                arrivals[4] = [from_below, from_above]
            hand_on(dz)

    def from_y(*groups):
        for dz in groups:
            over_y[dz].wait_recv()
            share(1, dz)

    for d in (2, -2, 1, -1):
        along(0, d)
    hand_on(0)

    for copy in vol_x + far:
        copy.wait_recv()
    features = jnp.concatenate([vol_full[i * 2 + p.yh] for i in range(NX)], axis=1)
    query_out[...] = jnp.dot(features, w_far[...], preferred_element_type=F32).astype(BF16)
    query_copy = net.start(query_out, query_in, p.across(0))
    from_z(6, 2)
    from_z(7, 1)
    near = [w_query[pl.ds(pl.multiple_of((i * 2 + p.yh) * 128, 128), 128), :] for i in range(NX)]
    query = jnp.dot(features, jnp.concatenate(near, axis=0), preferred_element_type=F32)
    from_y(0, 6, 2, 7, 1)
    from_z(5, 3)
    from_z(4)
    vol_y = net.start(vol, vol_full.at[h], p.across(0))
    query_copy.wait_recv()
    query = (query + query_in[...].astype(F32)).astype(BF16)
    place(0, query.astype(F32) * scale)

    def scan(dz):
        at = pl.ds(pl.multiple_of(dz * group, group), group)
        x[at, :] = jnp.dot(kv[dz].reshape(group, 256), mt[...], preferred_element_type=F32)
        for j in range(tiles):
            cols = slice(j * 128, j * 128 + 128)
            scores = x[at, cols].reshape(group // 8, 8, 128)
            dprob = x[at, pair + j * 128 : pair + j * 128 + 128].reshape(group // 8, 8, 128)
            before = top[:, cols]
            now = jnp.maximum(before, jnp.max(scores, axis=0))
            expo = jnp.exp(scores - now[None])
            fade = jnp.exp(before - now)
            top[:, cols] = now
            total[:, cols] = total[:, cols] * fade + jnp.sum(expo, axis=0)
            weighted[:, cols] = weighted[:, cols] * fade + jnp.sum(expo * dprob, axis=0)

    def have(*groups):
        for dz in groups:
            shared[0, dz].wait_recv()
            shared[1, dz].wait_recv()

    have(0)
    scan(0)
    have(6)
    scan(6)
    from_y(5, 3)
    have(2)
    scan(2)
    from_y(4)
    quarter = p.c * 2 + p.yl
    surf_quad[0] = surf_full[pl.ds(quarter * 2, 2)]
    squares = []
    for slot, device, its in (
        (3, p.diagonal(), (1 - p.c) * 2 + 1 - p.yl),
        (2, p.other_yl(), p.c * 2 + 1 - p.yl),
        (1, p.sibling(), (1 - p.c) * 2 + p.yl),
    ):
        squares.append(net.start(surf_full.at[pl.ds(its * 2, 2)], surf_quad.at[slot], device))
    have(7, 1)
    scan(7)
    scan(1)
    have(5, 3)
    scan(5)
    scan(3)
    vol_y.wait_recv()
    vol_x = [net.start(vol_full.at[hp], vol_full.at[hp], p.along_x(d)) for d in (2, 1, 3)]
    have(4)
    scan(4)

    best = jnp.max(top[...], axis=0, keepdims=True)
    fade = jnp.exp(top[...] - best)
    sums = jnp.sum(total[...] * fade, axis=0, keepdims=True)
    delta = jnp.sum(weighted[...] * fade, axis=0, keepdims=True) / sums
    top[...] = jnp.broadcast_to(best, top.shape)
    total[...] = jnp.broadcast_to(jnp.log(sums), total.shape)
    weighted[...] = jnp.broadcast_to(delta, weighted.shape)
    dqt[...] = jnp.zeros_like(dqt)

    def grads(dz):
        at = pl.ds(pl.multiple_of(dz * group, group), group)
        for j in range(tiles):
            cols = slice(j * 128, j * 128 + 128)
            more = slice(pair + j * 128, pair + j * 128 + 128)
            scores = x[at, cols].reshape(group // 8, 8, 128)
            dprob = x[at, more].reshape(group // 8, 8, 128)
            probs = jnp.exp((scores - top[:, cols][None]) - total[:, cols][None])
            dscore = probs * (dprob - weighted[:, cols][None])
            y[:, cols] = dscore.reshape(group, 128).astype(BF16)
            y[:, more] = probs.reshape(group, 128).astype(BF16)
        both = jnp.dot(y[...], m[...], preferred_element_type=F32)
        part[dz] = both.astype(BF16).reshape(2, 2, ctx, 256)
        keys = kv[dz].reshape(group, 256)[:, 0:128]
        dqt[...] += lax.dot_general(keys, y[:, 0:pair], TN, preferred_element_type=F32)

    sib = {}
    from_yl = {}
    from_peer = []

    def to_sibling(dz):
        sib[dz] = net.start(part.at[dz, 1], sib_in.at[dz], p.sibling())

    def chip_sum(t, dz):
        return part[dz, 0, t].astype(F32) + sib_in[dz, t].astype(F32)

    def to_y(dz):
        sib[dz].wait_recv()
        yl_out[dz] = chip_sum(1, dz).astype(BF16)
        from_yl[dz] = net.start(yl_out.at[dz], yl_in.at[dz], p.other_yl())

    def both_sum(dz):
        from_yl[dz].wait_recv()
        return chip_sum(0, dz) + yl_in[dz].astype(F32)

    def to_peer(dz):
        value = both_sum(dz)
        z_sums[dz] = value.astype(BF16)
        block = z_sums.at[dz]
        if dz == 4:
            stepped["half", 6] = net.start(block.at[upper], half_in.at[0], p.along_z(-2))
            stepped["half", 2] = net.start(block.at[lower], half_in.at[1], p.along_z(2))
        elif dz == 5:
            stepped["whole", 6] = net.start(block, step_in.at[0], p.along_z(-1))
        elif dz == 3:
            stepped["whole", 2] = net.start(block, step_in.at[1], p.along_z(1))
        elif dz in (7, 1):
            ended.append(net.start(block, end_in.at[len(ended)], p.along_z(1 if dz == 1 else -1)))

    def to_owner(dz):
        side, rows_of = (0, upper) if dz == 6 else (1, lower)
        value = both_sum(dz)
        stepped["whole", dz].wait_recv()
        z_sums[dz] = (value + step_in[side].astype(F32)).astype(BF16)
        stepped["half", dz].wait_recv()
        z_sums[dz, rows_of] = (z_sums[dz, rows_of].astype(F32) + half_in[side].astype(F32)).astype(BF16)
        ended.append(net.start(z_sums.at[dz], end_in.at[len(ended)], p.along_z(2 if dz == 2 else -2)))

    stepped = {}
    ended = []
    order = (4, 5, 3, 6, 2, 7, 1, 0)
    for i, dz in enumerate(order):
        grads(dz)
        to_sibling(dz)
        if i >= 2:
            to_y(order[i - 2])
        if i >= 5:
            to_peer(order[i - 5])

    to_y(1)
    to_owner(6)
    to_y(0)
    to_owner(2)
    turned = jnp.concatenate([dqt[0:HEAD_DIM, 0:rows], dqt[HEAD_DIM:128, rows:pair]], axis=0) * scale
    dq = turned.T.astype(BF16)
    turned = turned.astype(BF16)
    to_peer(7)
    to_peer(1)

    for i in range(NX):
        vol_out[i] = lax.dot_general(dq, w_query[i * 256 : i * 256 + 256, :], NT, preferred_element_type=F32).astype(BF16)
    for copy in vol_x:
        copy.wait_recv()
    vol_x = [net.start(vol_out.at[(p.x + d) % NX], vol_in.at[d - 1], p.along_x(d)) for d in (2, 1, 3)]
    for i in range(4):
        block = jnp.concatenate([vol_full[2 * i], vol_full[2 * i + 1]], axis=1)
        q_part[i // 2, i % 2] = jnp.dot(turned, block, preferred_element_type=F32).astype(BF16)
    q_sib = net.start(q_part.at[1 - p.c], q_core, p.sibling())

    own = both_sum(0)
    for i, copy in enumerate(ended):
        copy.wait_recv()
        own = own + end_in[i].astype(F32)
    dkv_quad[0] = own.astype(BF16)
    dkv_copies = [net.start(dkv_quad.at[0], dkv_quad.at[3 - i], square[i]) for i in range(3)]
    q_sib.wait_recv()
    q_yl[...] = (q_part[p.c].astype(F32) + q_core[...].astype(F32)).astype(BF16)
    q_copy = net.start(q_yl.at[1 - p.yl], q_yl_in, p.other_yl())
    dkv = dkv_quad[0]
    for i in range(NX):
        weights = jnp.concatenate([w_key[i * 256 : i * 256 + 256, :], w_value[i * 256 : i * 256 + 256, :]], axis=1)
        surf_out[i] = lax.dot_general(dkv, weights, NT, preferred_element_type=F32).astype(BF16)
    surf_x = [net.start(surf_out.at[(p.x + d) % NX], surf_in.at[d - 1], p.along_x(d)) for d in (2, 1, 3)]
    q_copy.wait_recv()
    z_out[:, :, 256:384] = (q_yl[p.yl].astype(F32) + q_yl_in[...].astype(F32)).T.reshape(NZ, 32, 128).astype(BF16)

    for copy in squares + dkv_copies:
        copy.wait_recv()
    dkv = dkv_quad[...].reshape(4 * ctx, 256)
    for i in range(2):
        points = jnp.concatenate([surf_quad[j, i] for j in range(4)], axis=0)
        block = lax.dot_general(points, dkv, TN, preferred_element_type=F32).astype(BF16)
        z_out[i * 4 : i * 4 + 4, :, 0:256] = block.reshape(4, 32, 256)

    far_first = (4, 3, 5, 2, 6, 1, 7)
    scattered = [net.start(z_out.at[(p.z + d) % NZ], z_in.at[d - 1], p.along_z(d)) for d in far_first]
    for copy in scattered:
        copy.wait_recv()
    sums = z_out[p.z].astype(F32)
    for i in range(NZ - 1):
        sums = sums + z_in[i].astype(F32)
    out[quarter, p.z] = sums.astype(BF16)

    def forward(dz):
        block = out.at[quarter, (p.z + dz) % NZ]
        return net.start(block, block, p.other_yl())

    mine = out.at[quarter, p.z]
    gathered = {d: net.start(mine, mine, p.along_z(d)) for d in far_first}
    forwarded = [forward(0)]

    def sum_x(copies, out, arrived, mid):
        for copy in copies:
            copy.wait_recv()
        sums = out[p.x].astype(F32)
        for i in range(NX - 1):
            sums = sums + arrived[i].astype(F32)
        mid[0] = sums[:, 0:128].astype(BF16)
        mid[1] = sums[:, 128:256].astype(BF16)

    sum_x(surf_x, surf_out, surf_in, surf_mid)
    surf_copy = net.start(surf_mid.at[1 - p.yh], surf_end, p.across(0))
    near_first = (1, 7, 2, 6, 3, 5, 4)
    for dz in near_first[0:4]:
        gathered[NZ - dz].wait_recv()
        forwarded.append(forward(dz))
    sum_x(vol_x, vol_out, vol_in, vol_mid)
    vol_copy = net.start(vol_mid.at[1 - p.yh], vol_end, p.across(0))
    for dz in near_first[4:]:
        gathered[NZ - dz].wait_recv()
        forwarded.append(forward(dz))
    to_core = [net.start(out.at[quarter], out.at[quarter], p.sibling())]
    for copy, dz in zip(forwarded, (0,) + near_first):
        copy.wait_recv()
        block = out.at[p.c * 2 + 1 - p.yl, (p.z + dz) % NZ]
        to_core.append(net.start(block, block, p.sibling()))
    surf_copy.wait_recv()
    grad_surf[...] = (surf_mid[p.yh].astype(F32) + surf_end[...].astype(F32)).astype(BF16)
    vol_copy.wait_recv()
    grad_vol[...] = (vol_mid[p.yh].astype(F32) + vol_end[...].astype(F32)).astype(BF16)
    for copy in to_core:
        copy.wait_recv()
    net.finish()


def finish_kernel(vol_in, surf_in, w_in, grad_vol, grad_surf, grad_wq, grad_wk, grad_wv):
    grad_vol[...] = vol_in[...]
    grad_surf[...] = surf_in[...]
    grad_wk[...] = w_in[:, 0:128].astype(F32)
    grad_wv[...] = w_in[:, 128:256].astype(F32)
    grad_wq[...] = w_in[:, 256:384].astype(F32)


def in_vmem(count):
    return [pl.BlockSpec(memory_space=pltpu.VMEM)] * count


def struct(*shape):
    return jax.ShapeDtypeStruct(shape, BF16)


def on_device(vol, surf, w_query, w_key, w_value, grad_out):
    rows, ctx = vol.shape[0], surf.shape[0]
    pair = 2 * rows
    group = 4 * ctx

    def over_x(n):
        return [
            pltpu.VMEM((NX, n, 256), BF16), pltpu.VMEM((NX - 1, n, 256), BF16),
            pltpu.VMEM((2, n, 128), BF16), pltpu.VMEM((n, 128), BF16),
        ]

    grad_vol, grad_surf, out = pl.pallas_call(
        whole_kernel,
        out_shape=[struct(rows, 128), struct(ctx, 128), struct(4, NZ, 32, 384)],
        in_specs=in_vmem(6),
        out_specs=in_vmem(3),
        scratch_shapes=[
            pltpu.VMEM((NZ, 2, 2, ctx, 256), BF16),
            pltpu.VMEM((8, rows, 128), BF16),
            pltpu.VMEM((8, ctx, 128), BF16),
            pltpu.VMEM((512, 128), BF16),
            pltpu.VMEM((rows, 128), BF16),
            pltpu.VMEM((rows, 128), BF16),
            pltpu.VMEM((4, 2, ctx, 128), BF16),
            pltpu.VMEM((4, ctx, 256), BF16),
            pltpu.VMEM((NZ * group, 2 * pair), F32),
            pltpu.VMEM((group, 2 * pair), BF16),
            pltpu.VMEM((2 * pair, 256), BF16),
            pltpu.VMEM((256, 2 * pair), BF16),
            pltpu.VMEM((128, pair), F32),
            pltpu.VMEM((8, pair), F32),
            pltpu.VMEM((8, pair), F32),
            pltpu.VMEM((8, pair), F32),
            pltpu.VMEM((NZ, 2, 2, ctx, 256), BF16),
            pltpu.VMEM((NZ, 2, ctx, 256), BF16),
            pltpu.VMEM((NZ, ctx, 256), BF16),
            pltpu.VMEM((NZ, ctx, 256), BF16),
            pltpu.VMEM((NZ, ctx, 256), BF16),
            pltpu.VMEM((2, ctx, 256), BF16),
            pltpu.VMEM((2, ctx // 2, 256), BF16),
            pltpu.VMEM((4, ctx, 256), BF16),
        ]
        + over_x(rows) + over_x(ctx)
        + [
            pltpu.VMEM((2, 2, 128, 256), BF16),
            pltpu.VMEM((2, 128, 256), BF16),
            pltpu.VMEM((2, 128, 256), BF16),
            pltpu.VMEM((128, 256), BF16),
            pltpu.VMEM((NZ, 32, 384), BF16),
            pltpu.VMEM((NZ - 1, 32, 384), BF16),
        ]
        + [pltpu.SemaphoreType.DMA((130,)), pltpu.SemaphoreType.DMA((130,))],
        compiler_params=pltpu.CompilerParams(collective_id=0, has_side_effects=True, vmem_limit_bytes=VMEM_LIMIT),
    )(vol, surf, w_query, w_key, w_value, grad_out)

    wide = jax.ShapeDtypeStruct((1024, 128), F32)
    return pl.pallas_call(
        finish_kernel,
        out_shape=[struct(rows, 128), struct(ctx, 128), wide, wide, wide],
        in_specs=in_vmem(3),
        out_specs=in_vmem(5),
    )(grad_vol, grad_surf, out.reshape(1024, 384))


def solution(mesh):
    in_specs = (
        P("blk", "heads"),
        P("blk", "heads"),
        P(None, "heads"),
        P(None, "heads"),
        P(None, "heads"),
        P("blk", "heads"),
    )
    out_specs = (
        P("blk", "heads"),
        P("blk", "heads"),
        P(None, "heads"),
        P(None, "heads"),
        P(None, "heads"),
    )
    return jax.shard_map(
        on_device, mesh=mesh, in_specs=in_specs, out_specs=out_specs, check_vma=False
    )
```

```python
import jax
import jax.numpy as jnp
from jax import lax
from jax.experimental import pallas as pl
from jax.experimental.pallas import tpu as pltpu
from jax.sharding import PartitionSpec as P

HEAD_DIM = 64
MESH = pl.DeviceIdType.MESH
VMEM_LIMIT = 60 * 1024 * 1024
F32 = jnp.float32
BF16 = jnp.bfloat16
NT = (((1,), (1,)), ((), ()))
TN = (((0,), (0,)), ((), ()))

NX, NZ = 4, 8


class Place:
    def __init__(self):
        self.h = lax.axis_index("heads")
        self.b = lax.axis_index("blk")
        self.x, self.yh = self.h // 2, self.h % 2
        self.yl, self.z, self.c = self.b // 16, (self.b // 2) % NZ, self.b % 2

    def along_x(self, d):
        return (((self.x + d) % NX) * 2 + self.yh, self.b)

    def across(self, d):
        return (((self.x + d) % NX) * 2 + 1 - self.yh, self.b)

    def along_z(self, d):
        return (self.h, self.yl * 16 + ((self.z + d) % NZ) * 2 + self.c)

    def other_yl(self):
        return (self.h, (1 - self.yl) * 16 + self.z * 2 + self.c)

    def sibling(self):
        return (self.h, self.yl * 16 + self.z * 2 + 1 - self.c)

    def diagonal(self):
        return (self.h, (1 - self.yl) * 16 + self.z * 2 + 1 - self.c)


def meet(partners):
    barrier = pltpu.get_barrier_semaphore()
    for partner in partners:
        pl.semaphore_signal(barrier, inc=1, device_id=partner, device_id_type=MESH)
    pl.semaphore_wait(barrier, len(partners))


class Sender:
    def __init__(self, send_sem, recv_sem):
        self.send_sem, self.recv_sem = send_sem, recv_sem
        self.used = 0
        self.all = []

    def start(self, src, dst, device):
        copy = pltpu.make_async_remote_copy(
            src_ref=src,
            dst_ref=dst,
            send_sem=self.send_sem.at[self.used],
            recv_sem=self.recv_sem.at[self.used],
            device_id=device,
            device_id_type=MESH,
        )
        self.used += 1
        copy.start()
        self.all.append(copy)
        return copy

    def finish(self):
        for copy in self.all:
            copy.wait_send()


def whole_kernel(
    vol, surf, w_query_in, w_key_in, w_value_in, grad_in,
    vol_result, surf_result, w_result,
    w_query, w_key, w_value, grad_out, grad_vol, grad_surf, out, local_sem,
    kv, vol_full, surf_full, w_far, query_out, query_in, surf_quad, dkv_quad, x, y, m, mt, dqt, top, total, weighted,
    part, sib_in, yl_out, yl_in, z_sums, step_in, half_in, end_in,
    vol_out, vol_in, vol_mid, vol_end, surf_out, surf_in, surf_mid, surf_end,
    q_part, q_core, q_yl, q_yl_in, z_out, z_in,
    send_sem, recv_sem,
):
    p = Place()
    h = p.h
    hp = p.x * 2 + 1 - p.yh
    rows, ctx = vol.shape[0], surf.shape[0]
    group = 4 * ctx
    pair = 2 * rows
    tiles = pair // 128
    scale = HEAD_DIM**-0.5
    heads = [p.across(d) for d in (2, 1, 3)] + [p.along_x(2), p.across(0), p.along_x(1), p.along_x(3)]
    square = [p.diagonal(), p.other_yl(), p.sibling()]
    held = []

    def hold(src, dst):
        held.append(pltpu.make_async_copy(src, dst, local_sem.at[len(held)]))
        held[-1].start()

    hold(grad_in, grad_out)
    hold(surf, surf_full.at[h])
    hold(w_key_in, w_key)
    hold(w_value_in, w_value)
    hold(vol, vol_full.at[h])
    hold(w_query_in, w_query)
    meet(heads + square + [p.along_z(d) for d in range(1, NZ)])
    net = Sender(send_sem, recv_sem)

    surf_all = [net.start(surf, surf_full.at[h], peer) for peer in heads]
    vol_x = [net.start(vol, vol_full.at[h], p.along_x(d)) for d in (2, 1, 3)]
    far = []
    for i in range(NX):
        rows_far = pl.ds(pl.multiple_of((i * 2 + 1 - p.yh) * 128, 128), 128)
        far.append(net.start(w_query_in.at[rows_far], w_far.at[pl.ds(i * 128, 128)], p.across(0)))

    def place(index, block):
        turned = block.T
        col = lax.broadcasted_iota(jnp.int32, block.shape, 1)
        row = lax.broadcasted_iota(jnp.int32, turned.shape, 0)
        for head in (0, 1):
            at = index * pair + head * rows
            m[at : at + rows, index * 128 : index * 128 + 128] = jnp.where(col // HEAD_DIM == head, block, 0.0).astype(BF16)
            mt[index * 128 : index * 128 + 128, at : at + rows] = jnp.where(row // HEAD_DIM == head, turned, 0.0).astype(BF16)

    m[...] = jnp.zeros_like(m)
    mt[...] = jnp.zeros_like(mt)
    for copy in held:
        copy.wait()
    place(1, grad_out[...].astype(F32))
    top[...] = jnp.full_like(top, -jnp.inf)
    total[...] = jnp.zeros_like(total)
    weighted[...] = jnp.zeros_like(weighted)

    for copy in surf_all:
        copy.wait_recv()
    features = jnp.concatenate([surf_full[i] for i in range(8)], axis=1)
    kv[0, 0, 0, :, 0:128] = jnp.dot(features, w_key[...], preferred_element_type=F32).astype(BF16)
    kv[0, 0, 0, :, 128:256] = jnp.dot(features, w_value[...], preferred_element_type=F32).astype(BF16)

    arrivals = {}
    over_y = {}
    shared = {}
    mid = ctx // 2
    upper, lower = slice(0, mid), slice(mid, ctx)

    def share(dz):
        shared[dz] = net.start(kv.at[dz, 0], kv.at[dz, 1], p.sibling())

    def along(dz, d):
        to = (dz - d) % NZ
        arrivals[to] = [net.start(kv.at[dz, 0, 0], kv.at[to, 0, 0], p.along_z(d))]

    def hand_on(dz):
        over_y[dz] = net.start(kv.at[dz, 0, 0], kv.at[dz, 0, 1], p.other_yl())

    def from_z(*groups):
        for dz in groups:
            for copy in arrivals[dz]:
                copy.wait_recv()
            if dz == 6:
                along(6, 1)
                from_below = net.start(kv.at[6, 0, 0, upper], kv.at[4, 0, 0, upper], p.along_z(2))
            if dz == 2:
                along(2, -1)
                from_above = net.start(kv.at[2, 0, 0, lower], kv.at[4, 0, 0, lower], p.along_z(-2))
                arrivals[4] = [from_below, from_above]
            hand_on(dz)

    def from_y(*groups):
        for dz in groups:
            over_y[dz].wait_recv()
            share(dz)

    for d in (2, -2, 1, -1):
        along(0, d)
    hand_on(0)

    for copy in vol_x + far:
        copy.wait_recv()
    features = jnp.concatenate([vol_full[i * 2 + p.yh] for i in range(NX)], axis=1)
    query_out[...] = jnp.dot(features, w_far[...], preferred_element_type=F32).astype(BF16)
    query_copy = net.start(query_out, query_in, p.across(0))
    from_z(6, 2)
    from_z(7, 1)
    near = [w_query[pl.ds(pl.multiple_of((i * 2 + p.yh) * 128, 128), 128), :] for i in range(NX)]
    query = jnp.dot(features, jnp.concatenate(near, axis=0), preferred_element_type=F32)
    from_y(0, 6, 2)
    from_z(5, 3)
    from_z(4)
    from_y(7, 1)
    vol_y = net.start(vol, vol_full.at[h], p.across(0))
    query_copy.wait_recv()
    query = (query + query_in[...].astype(F32)).astype(BF16)
    place(0, query.astype(F32) * scale)

    def scan(dz):
        at = pl.ds(pl.multiple_of(dz * group, group), group)
        x[at, :] = jnp.dot(kv[dz].reshape(group, 256), mt[...], preferred_element_type=F32)
        for j in range(tiles):
            cols = slice(j * 128, j * 128 + 128)
            scores = x[at, cols].reshape(group // 8, 8, 128)
            dprob = x[at, pair + j * 128 : pair + j * 128 + 128].reshape(group // 8, 8, 128)
            before = top[:, cols]
            now = jnp.maximum(before, jnp.max(scores, axis=0))
            expo = jnp.exp(scores - now[None])
            fade = jnp.exp(before - now)
            top[:, cols] = now
            total[:, cols] = total[:, cols] * fade + jnp.sum(expo, axis=0)
            weighted[:, cols] = weighted[:, cols] * fade + jnp.sum(expo * dprob, axis=0)

    def have(*groups):
        for dz in groups:
            shared[dz].wait_recv()

    have(0)
    scan(0)
    have(6)
    scan(6)
    from_y(5, 3)
    have(2)
    scan(2)
    from_y(4)
    quarter = p.c * 2 + p.yl
    surf_quad[0] = surf_full[pl.ds(quarter * 2, 2)]
    squares = []
    for slot, device, its in (
        (3, p.diagonal(), (1 - p.c) * 2 + 1 - p.yl),
        (2, p.other_yl(), p.c * 2 + 1 - p.yl),
        (1, p.sibling(), (1 - p.c) * 2 + p.yl),
    ):
        squares.append(net.start(surf_full.at[pl.ds(its * 2, 2)], surf_quad.at[slot], device))
    have(7, 1)
    scan(7)
    scan(1)
    have(5, 3)
    scan(5)
    scan(3)
    vol_y.wait_recv()
    vol_x = [net.start(vol_full.at[hp], vol_full.at[hp], p.along_x(d)) for d in (2, 1, 3)]
    have(4)
    scan(4)

    best = jnp.max(top[...], axis=0, keepdims=True)
    fade = jnp.exp(top[...] - best)
    sums = jnp.sum(total[...] * fade, axis=0, keepdims=True)
    delta = jnp.sum(weighted[...] * fade, axis=0, keepdims=True) / sums
    top[...] = jnp.broadcast_to(best, top.shape)
    total[...] = jnp.broadcast_to(jnp.log(sums), total.shape)
    weighted[...] = jnp.broadcast_to(delta, weighted.shape)
    dqt[...] = jnp.zeros_like(dqt)

    def grads(dz):
        at = pl.ds(pl.multiple_of(dz * group, group), group)
        for j in range(tiles):
            cols = slice(j * 128, j * 128 + 128)
            more = slice(pair + j * 128, pair + j * 128 + 128)
            scores = x[at, cols].reshape(group // 8, 8, 128)
            dprob = x[at, more].reshape(group // 8, 8, 128)
            probs = jnp.exp((scores - top[:, cols][None]) - total[:, cols][None])
            dscore = probs * (dprob - weighted[:, cols][None])
            y[:, cols] = dscore.reshape(group, 128).astype(BF16)
            y[:, more] = probs.reshape(group, 128).astype(BF16)
        both = jnp.dot(y[...], m[...], preferred_element_type=F32)
        part[dz] = both.astype(BF16).reshape(2, 2, ctx, 256)
        keys = kv[dz].reshape(group, 256)[:, 0:128]
        dqt[...] += lax.dot_general(keys, y[:, 0:pair], TN, preferred_element_type=F32)

    sib = {}
    from_yl = {}
    from_peer = []

    def to_sibling(dz):
        sib[dz] = net.start(part.at[dz, 1], sib_in.at[dz], p.sibling())

    def chip_sum(t, dz):
        return part[dz, 0, t].astype(F32) + sib_in[dz, t].astype(F32)

    def to_y(dz):
        sib[dz].wait_recv()
        yl_out[dz] = chip_sum(1, dz).astype(BF16)
        from_yl[dz] = net.start(yl_out.at[dz], yl_in.at[dz], p.other_yl())

    def both_sum(dz):
        from_yl[dz].wait_recv()
        return chip_sum(0, dz) + yl_in[dz].astype(F32)

    def to_peer(dz):
        value = both_sum(dz)
        z_sums[dz] = value.astype(BF16)
        block = z_sums.at[dz]
        if dz == 4:
            stepped["half", 6] = net.start(block.at[upper], half_in.at[0], p.along_z(-2))
            stepped["half", 2] = net.start(block.at[lower], half_in.at[1], p.along_z(2))
        elif dz == 5:
            stepped["whole", 6] = net.start(block, step_in.at[0], p.along_z(-1))
        elif dz == 3:
            stepped["whole", 2] = net.start(block, step_in.at[1], p.along_z(1))
        elif dz in (7, 1):
            ended.append(net.start(block, end_in.at[len(ended)], p.along_z(1 if dz == 1 else -1)))

    def to_owner(dz):
        side, rows_of = (0, upper) if dz == 6 else (1, lower)
        value = both_sum(dz)
        stepped["whole", dz].wait_recv()
        z_sums[dz] = (value + step_in[side].astype(F32)).astype(BF16)
        stepped["half", dz].wait_recv()
        z_sums[dz, rows_of] = (z_sums[dz, rows_of].astype(F32) + half_in[side].astype(F32)).astype(BF16)
        ended.append(net.start(z_sums.at[dz], end_in.at[len(ended)], p.along_z(2 if dz == 2 else -2)))

    stepped = {}
    ended = []
    order = (4, 5, 3, 6, 2, 7, 1, 0)
    for i, dz in enumerate(order):
        grads(dz)
        to_sibling(dz)
        if i >= 2:
            to_y(order[i - 2])
        if i >= 5:
            to_peer(order[i - 5])

    to_y(1)
    to_owner(6)
    to_y(0)
    to_owner(2)
    turned = jnp.concatenate([dqt[0:HEAD_DIM, 0:rows], dqt[HEAD_DIM:128, rows:pair]], axis=0) * scale
    dq = turned.T.astype(BF16)
    turned = turned.astype(BF16)
    to_peer(7)
    to_peer(1)

    for i in range(NX):
        vol_out[i] = lax.dot_general(dq, w_query[i * 256 : i * 256 + 256, :], NT, preferred_element_type=F32).astype(BF16)
    for copy in vol_x:
        copy.wait_recv()
    vol_x = [net.start(vol_out.at[(p.x + d) % NX], vol_in.at[d - 1], p.along_x(d)) for d in (2, 1, 3)]
    for i in range(4):
        block = jnp.concatenate([vol_full[2 * i], vol_full[2 * i + 1]], axis=1)
        q_part[i // 2, i % 2] = jnp.dot(turned, block, preferred_element_type=F32).astype(BF16)
    q_sib = net.start(q_part.at[1 - p.c], q_core, p.sibling())

    own = both_sum(0)
    for i, copy in enumerate(ended):
        copy.wait_recv()
        own = own + end_in[i].astype(F32)
    dkv_quad[0] = own.astype(BF16)
    dkv_copies = [net.start(dkv_quad.at[0], dkv_quad.at[3 - i], square[i]) for i in range(3)]
    q_sib.wait_recv()
    q_yl[...] = (q_part[p.c].astype(F32) + q_core[...].astype(F32)).astype(BF16)
    q_copy = net.start(q_yl.at[1 - p.yl], q_yl_in, p.other_yl())
    dkv = dkv_quad[0]
    for i in range(NX):
        weights = jnp.concatenate([w_key[i * 256 : i * 256 + 256, :], w_value[i * 256 : i * 256 + 256, :]], axis=1)
        surf_out[i] = lax.dot_general(dkv, weights, NT, preferred_element_type=F32).astype(BF16)
    surf_x = [net.start(surf_out.at[(p.x + d) % NX], surf_in.at[d - 1], p.along_x(d)) for d in (2, 1, 3)]
    q_copy.wait_recv()
    z_out[:, :, 256:384] = (q_yl[p.yl].astype(F32) + q_yl_in[...].astype(F32)).T.reshape(NZ, 32, 128).astype(BF16)

    for copy in squares + dkv_copies:
        copy.wait_recv()
    dkv = dkv_quad[...].reshape(4 * ctx, 256)
    for i in range(2):
        points = jnp.concatenate([surf_quad[j, i] for j in range(4)], axis=0)
        block = lax.dot_general(points, dkv, TN, preferred_element_type=F32).astype(BF16)
        z_out[i * 4 : i * 4 + 4, :, 0:256] = block.reshape(4, 32, 256)

    far_first = (4, 3, 5, 2, 6, 1, 7)
    scattered = [net.start(z_out.at[(p.z + d) % NZ], z_in.at[d - 1], p.along_z(d)) for d in far_first]
    for copy in scattered:
        copy.wait_recv()
    sums = z_out[p.z].astype(F32)
    for i in range(NZ - 1):
        sums = sums + z_in[i].astype(F32)
    out[quarter, p.z] = sums.astype(BF16)

    def forward(dz):
        block = out.at[quarter, (p.z + dz) % NZ]
        return net.start(block, block, p.other_yl())

    mine = out.at[quarter, p.z]
    gathered = {d: net.start(mine, mine, p.along_z(d)) for d in far_first}
    forwarded = [forward(0)]

    def sum_x(copies, out, arrived, mid):
        for copy in copies:
            copy.wait_recv()
        sums = out[p.x].astype(F32)
        for i in range(NX - 1):
            sums = sums + arrived[i].astype(F32)
        mid[0] = sums[:, 0:128].astype(BF16)
        mid[1] = sums[:, 128:256].astype(BF16)

    sum_x(surf_x, surf_out, surf_in, surf_mid)
    surf_copy = net.start(surf_mid.at[1 - p.yh], surf_end, p.across(0))
    near_first = (1, 7, 2, 6, 3, 5, 4)
    for dz in near_first[0:4]:
        gathered[NZ - dz].wait_recv()
        forwarded.append(forward(dz))
    sum_x(vol_x, vol_out, vol_in, vol_mid)
    vol_copy = net.start(vol_mid.at[1 - p.yh], vol_end, p.across(0))
    for dz in near_first[4:]:
        gathered[NZ - dz].wait_recv()
        forwarded.append(forward(dz))
    to_core = [net.start(out.at[quarter], out.at[quarter], p.sibling())]
    hold(out.at[quarter], w_result.at[quarter])
    for copy, dz in zip(forwarded, (0,) + near_first):
        copy.wait_recv()
        block = out.at[p.c * 2 + 1 - p.yl, (p.z + dz) % NZ]
        to_core.append(net.start(block, block, p.sibling()))
    theirs = p.c * 2 + 1 - p.yl
    hold(out.at[theirs], w_result.at[theirs])
    surf_copy.wait_recv()
    grad_surf[...] = (surf_mid[p.yh].astype(F32) + surf_end[...].astype(F32)).astype(BF16)
    vol_copy.wait_recv()
    grad_vol[...] = (vol_mid[p.yh].astype(F32) + vol_end[...].astype(F32)).astype(BF16)
    hold(grad_vol, vol_result)
    hold(grad_surf, surf_result)
    for copy in to_core:
        copy.wait_recv()
    side = pl.ds((1 - p.c) * 2, 2)
    hold(out.at[side], w_result.at[side])
    for copy in held[6:]:
        copy.wait()
    net.finish()


def finish_kernel(vol_in, surf_in, w_in, grad_vol, grad_surf, grad_wq, grad_wk, grad_wv):
    grad_vol[...] = vol_in[...]
    grad_surf[...] = surf_in[...]
    grad_wk[...] = w_in[:, 0:128].astype(F32)
    grad_wv[...] = w_in[:, 128:256].astype(F32)
    grad_wq[...] = w_in[:, 256:384].astype(F32)


def in_vmem(count):
    return [pl.BlockSpec(memory_space=pltpu.VMEM)] * count


def struct(*shape):
    return jax.ShapeDtypeStruct(shape, BF16)


def on_device(vol, surf, w_query, w_key, w_value, grad_out):
    rows, ctx = vol.shape[0], surf.shape[0]
    pair = 2 * rows
    group = 4 * ctx

    def over_x(n):
        return [
            pltpu.VMEM((NX, n, 256), BF16), pltpu.VMEM((NX - 1, n, 256), BF16),
            pltpu.VMEM((2, n, 128), BF16), pltpu.VMEM((n, 128), BF16),
        ]

    grad_vol, grad_surf, out = pl.pallas_call(
        whole_kernel,
        out_shape=[struct(rows, 128), struct(ctx, 128), struct(4, NZ, 32, 384)],
        in_specs=[pl.BlockSpec(memory_space=pl.ANY)] * 6,
        out_specs=[pl.BlockSpec(memory_space=pl.ANY)] * 3,
        scratch_shapes=[
            pltpu.VMEM((1024, 128), BF16),
            pltpu.VMEM((1024, 128), BF16),
            pltpu.VMEM((1024, 128), BF16),
            pltpu.VMEM((rows, 128), BF16),
            pltpu.VMEM((rows, 128), BF16),
            pltpu.VMEM((ctx, 128), BF16),
            pltpu.VMEM((4, NZ, 32, 384), BF16),
            pltpu.SemaphoreType.DMA((12,)),
            pltpu.VMEM((NZ, 2, 2, ctx, 256), BF16),
            pltpu.VMEM((8, rows, 128), BF16),
            pltpu.VMEM((8, ctx, 128), BF16),
            pltpu.VMEM((512, 128), BF16),
            pltpu.VMEM((rows, 128), BF16),
            pltpu.VMEM((rows, 128), BF16),
            pltpu.VMEM((4, 2, ctx, 128), BF16),
            pltpu.VMEM((4, ctx, 256), BF16),
            pltpu.VMEM((NZ * group, 2 * pair), F32),
            pltpu.VMEM((group, 2 * pair), BF16),
            pltpu.VMEM((2 * pair, 256), BF16),
            pltpu.VMEM((256, 2 * pair), BF16),
            pltpu.VMEM((128, pair), F32),
            pltpu.VMEM((8, pair), F32),
            pltpu.VMEM((8, pair), F32),
            pltpu.VMEM((8, pair), F32),
            pltpu.VMEM((NZ, 2, 2, ctx, 256), BF16),
            pltpu.VMEM((NZ, 2, ctx, 256), BF16),
            pltpu.VMEM((NZ, ctx, 256), BF16),
            pltpu.VMEM((NZ, ctx, 256), BF16),
            pltpu.VMEM((NZ, ctx, 256), BF16),
            pltpu.VMEM((2, ctx, 256), BF16),
            pltpu.VMEM((2, ctx // 2, 256), BF16),
            pltpu.VMEM((4, ctx, 256), BF16),
        ]
        + over_x(rows) + over_x(ctx)
        + [
            pltpu.VMEM((2, 2, 128, 256), BF16),
            pltpu.VMEM((2, 128, 256), BF16),
            pltpu.VMEM((2, 128, 256), BF16),
            pltpu.VMEM((128, 256), BF16),
            pltpu.VMEM((NZ, 32, 384), BF16),
            pltpu.VMEM((NZ - 1, 32, 384), BF16),
        ]
        + [pltpu.SemaphoreType.DMA((130,)), pltpu.SemaphoreType.DMA((130,))],
        compiler_params=pltpu.CompilerParams(collective_id=0, has_side_effects=True, vmem_limit_bytes=VMEM_LIMIT),
    )(vol, surf, w_query, w_key, w_value, grad_out)

    wide = jax.ShapeDtypeStruct((1024, 128), F32)
    return pl.pallas_call(
        finish_kernel,
        out_shape=[struct(rows, 128), struct(ctx, 128), wide, wide, wide],
        in_specs=in_vmem(3),
        out_specs=in_vmem(5),
    )(grad_vol, grad_surf, out.reshape(1024, 384))


def solution(mesh):
    in_specs = (
        P("blk", "heads"),
        P("blk", "heads"),
        P(None, "heads"),
        P(None, "heads"),
        P(None, "heads"),
        P("blk", "heads"),
    )
    out_specs = (
        P("blk", "heads"),
        P("blk", "heads"),
        P(None, "heads"),
        P(None, "heads"),
        P(None, "heads"),
    )
    return jax.shard_map(
        on_device, mesh=mesh, in_specs=in_specs, out_specs=out_specs, check_vma=False
    )
```

```python
import jax
import jax.numpy as jnp
from jax import lax
from jax.experimental import pallas as pl
from jax.experimental.pallas import tpu as pltpu
from jax.sharding import PartitionSpec as P

HEAD_DIM = 64
MESH = pl.DeviceIdType.MESH
VMEM_LIMIT = 60 * 1024 * 1024
F32 = jnp.float32
BF16 = jnp.bfloat16
NT = (((1,), (1,)), ((), ()))
TN = (((0,), (0,)), ((), ()))

NX, NZ = 4, 8


class Place:
    def __init__(self):
        self.h = lax.axis_index("heads")
        self.b = lax.axis_index("blk")
        self.x, self.yh = self.h // 2, self.h % 2
        self.yl, self.z, self.c = self.b // 16, (self.b // 2) % NZ, self.b % 2

    def along_x(self, d):
        return (((self.x + d) % NX) * 2 + self.yh, self.b)

    def across(self, d):
        return (((self.x + d) % NX) * 2 + 1 - self.yh, self.b)

    def along_z(self, d):
        return (self.h, self.yl * 16 + ((self.z + d) % NZ) * 2 + self.c)

    def other_yl(self):
        return (self.h, (1 - self.yl) * 16 + self.z * 2 + self.c)

    def sibling(self):
        return (self.h, self.yl * 16 + self.z * 2 + 1 - self.c)

    def diagonal(self):
        return (self.h, (1 - self.yl) * 16 + self.z * 2 + 1 - self.c)


def meet(partners):
    barrier = pltpu.get_barrier_semaphore()
    for partner in partners:
        pl.semaphore_signal(barrier, inc=1, device_id=partner, device_id_type=MESH)
    pl.semaphore_wait(barrier, len(partners))


class Sender:
    def __init__(self, send_sem, recv_sem):
        self.send_sem, self.recv_sem = send_sem, recv_sem
        self.used = 0
        self.all = []

    def start(self, src, dst, device):
        copy = pltpu.make_async_remote_copy(
            src_ref=src,
            dst_ref=dst,
            send_sem=self.send_sem.at[self.used],
            recv_sem=self.recv_sem.at[self.used],
            device_id=device,
            device_id_type=MESH,
        )
        self.used += 1
        copy.start()
        self.all.append(copy)
        return copy

    def finish(self):
        for copy in self.all:
            copy.wait_send()


def whole_kernel(
    vol, surf, w_query_in, w_key_in, w_value_in, grad_in,
    vol_result, surf_result, w_result,
    w_query, w_key, w_value, grad_out, grad_vol, grad_surf, out, local_sem,
    kv, vol_full, surf_full, w_far, query_out, query_in, surf_quad, dkv_quad, x, y, m, mt, dqt, top, total, weighted,
    part, sib_in, yl_out, yl_in, z_sums, step_in, half_in, end_in,
    w_rows, dq_full, surf_out, surf_in, surf_mid, surf_end,
    q_part, q_core, q_yl, q_yl_in, z_out, z_in,
    send_sem, recv_sem,
):
    p = Place()
    h = p.h
    hp = p.x * 2 + 1 - p.yh
    rows, ctx = vol.shape[0], surf.shape[0]
    group = 4 * ctx
    pair = 2 * rows
    tiles = pair // 128
    scale = HEAD_DIM**-0.5
    heads = [p.across(d) for d in (2, 1, 3)] + [p.along_x(2), p.across(0), p.along_x(1), p.along_x(3)]
    square = [p.diagonal(), p.other_yl(), p.sibling()]
    held = []

    def hold(src, dst):
        held.append(pltpu.make_async_copy(src, dst, local_sem.at[len(held)]))
        held[-1].start()

    hold(grad_in, grad_out)
    hold(surf, surf_full.at[h])
    hold(w_key_in, w_key)
    hold(w_value_in, w_value)
    hold(vol, vol_full.at[h])
    hold(w_query_in, w_query)
    meet(heads + square + [p.along_z(d) for d in range(1, NZ)])
    net = Sender(send_sem, recv_sem)

    surf_all = [net.start(surf, surf_full.at[h], peer) for peer in heads]
    vol_x = [net.start(vol, vol_full.at[h], p.along_x(d)) for d in (2, 1, 3)]
    far = []
    for i in range(NX):
        rows_far = pl.ds(pl.multiple_of((i * 2 + 1 - p.yh) * 128, 128), 128)
        far.append(net.start(w_query_in.at[rows_far], w_far.at[pl.ds(i * 128, 128)], p.across(0)))

    def place(index, block):
        turned = block.T
        col = lax.broadcasted_iota(jnp.int32, block.shape, 1)
        row = lax.broadcasted_iota(jnp.int32, turned.shape, 0)
        for head in (0, 1):
            at = index * pair + head * rows
            m[at : at + rows, index * 128 : index * 128 + 128] = jnp.where(col // HEAD_DIM == head, block, 0.0).astype(BF16)
            mt[index * 128 : index * 128 + 128, at : at + rows] = jnp.where(row // HEAD_DIM == head, turned, 0.0).astype(BF16)

    m[...] = jnp.zeros_like(m)
    mt[...] = jnp.zeros_like(mt)
    for copy in held:
        copy.wait()
    place(1, grad_out[...].astype(F32))
    top[...] = jnp.full_like(top, -jnp.inf)
    total[...] = jnp.zeros_like(total)
    weighted[...] = jnp.zeros_like(weighted)

    for copy in surf_all:
        copy.wait_recv()
    features = jnp.concatenate([surf_full[i] for i in range(8)], axis=1)
    kv[0, 0, 0, :, 0:128] = jnp.dot(features, w_key[...], preferred_element_type=F32).astype(BF16)
    kv[0, 0, 0, :, 128:256] = jnp.dot(features, w_value[...], preferred_element_type=F32).astype(BF16)

    arrivals = {}
    over_y = {}
    shared = {}
    mid = ctx // 2
    upper, lower = slice(0, mid), slice(mid, ctx)

    def share(dz):
        shared[dz] = net.start(kv.at[dz, 0], kv.at[dz, 1], p.sibling())

    def along(dz, d):
        to = (dz - d) % NZ
        arrivals[to] = [net.start(kv.at[dz, 0, 0], kv.at[to, 0, 0], p.along_z(d))]

    def hand_on(dz):
        over_y[dz] = net.start(kv.at[dz, 0, 0], kv.at[dz, 0, 1], p.other_yl())

    def from_z(*groups):
        for dz in groups:
            for copy in arrivals[dz]:
                copy.wait_recv()
            if dz == 6:
                along(6, 1)
                from_below = net.start(kv.at[6, 0, 0, upper], kv.at[4, 0, 0, upper], p.along_z(2))
            if dz == 2:
                along(2, -1)
                from_above = net.start(kv.at[2, 0, 0, lower], kv.at[4, 0, 0, lower], p.along_z(-2))
                arrivals[4] = [from_below, from_above]
            hand_on(dz)

    def from_y(*groups):
        for dz in groups:
            over_y[dz].wait_recv()
            share(dz)

    for d in (2, -2, 1, -1):
        along(0, d)
    hand_on(0)

    for copy in vol_x + far:
        copy.wait_recv()
    features = jnp.concatenate([vol_full[i * 2 + p.yh] for i in range(NX)], axis=1)
    query_out[...] = jnp.dot(features, w_far[...], preferred_element_type=F32).astype(BF16)
    query_copy = net.start(query_out, query_in, p.across(0))
    from_z(6, 2)
    from_z(7, 1)
    near = [w_query[pl.ds(pl.multiple_of((i * 2 + p.yh) * 128, 128), 128), :] for i in range(NX)]
    query = jnp.dot(features, jnp.concatenate(near, axis=0), preferred_element_type=F32)
    from_y(0, 6, 2)
    from_z(5, 3)
    from_z(4)
    from_y(7, 1)
    vol_y = net.start(vol, vol_full.at[h], p.across(0))
    query_copy.wait_recv()
    query = (query + query_in[...].astype(F32)).astype(BF16)
    place(0, query.astype(F32) * scale)

    def scan(dz):
        at = pl.ds(pl.multiple_of(dz * group, group), group)
        x[at, :] = jnp.dot(kv[dz].reshape(group, 256), mt[...], preferred_element_type=F32)
        for j in range(tiles):
            cols = slice(j * 128, j * 128 + 128)
            scores = x[at, cols].reshape(group // 8, 8, 128)
            dprob = x[at, pair + j * 128 : pair + j * 128 + 128].reshape(group // 8, 8, 128)
            before = top[:, cols]
            now = jnp.maximum(before, jnp.max(scores, axis=0))
            expo = jnp.exp(scores - now[None])
            fade = jnp.exp(before - now)
            top[:, cols] = now
            total[:, cols] = total[:, cols] * fade + jnp.sum(expo, axis=0)
            weighted[:, cols] = weighted[:, cols] * fade + jnp.sum(expo * dprob, axis=0)

    def have(*groups):
        for dz in groups:
            shared[dz].wait_recv()

    have(0)
    scan(0)
    have(6)
    scan(6)
    from_y(5, 3)
    have(2)
    scan(2)
    from_y(4)
    quarter = p.c * 2 + p.yl
    surf_quad[0] = surf_full[pl.ds(quarter * 2, 2)]
    squares = []
    for slot, device, its in (
        (3, p.diagonal(), (1 - p.c) * 2 + 1 - p.yl),
        (2, p.other_yl(), p.c * 2 + 1 - p.yl),
        (1, p.sibling(), (1 - p.c) * 2 + p.yl),
    ):
        squares.append(net.start(surf_full.at[pl.ds(its * 2, 2)], surf_quad.at[slot], device))
    w_rows[h] = w_query[pl.ds(pl.multiple_of(h * 128, 128), 128), :]
    swapped = []
    for peer in heads:
        its_rows = pl.ds(pl.multiple_of(peer[0] * 128, 128), 128)
        swapped.append(net.start(w_query.at[its_rows], w_rows.at[h], peer))
    have(7, 1)
    scan(7)
    scan(1)
    have(5, 3)
    scan(5)
    scan(3)
    vol_y.wait_recv()
    vol_x = [net.start(vol_full.at[hp], vol_full.at[hp], p.along_x(d)) for d in (2, 1, 3)]
    have(4)
    scan(4)

    best = jnp.max(top[...], axis=0, keepdims=True)
    fade = jnp.exp(top[...] - best)
    sums = jnp.sum(total[...] * fade, axis=0, keepdims=True)
    delta = jnp.sum(weighted[...] * fade, axis=0, keepdims=True) / sums
    top[...] = jnp.broadcast_to(best, top.shape)
    total[...] = jnp.broadcast_to(jnp.log(sums), total.shape)
    weighted[...] = jnp.broadcast_to(delta, weighted.shape)
    dqt[...] = jnp.zeros_like(dqt)

    def grads(dz):
        at = pl.ds(pl.multiple_of(dz * group, group), group)
        for j in range(tiles):
            cols = slice(j * 128, j * 128 + 128)
            more = slice(pair + j * 128, pair + j * 128 + 128)
            scores = x[at, cols].reshape(group // 8, 8, 128)
            dprob = x[at, more].reshape(group // 8, 8, 128)
            probs = jnp.exp((scores - top[:, cols][None]) - total[:, cols][None])
            dscore = probs * (dprob - weighted[:, cols][None])
            y[:, cols] = dscore.reshape(group, 128).astype(BF16)
            y[:, more] = probs.reshape(group, 128).astype(BF16)
        both = jnp.dot(y[...], m[...], preferred_element_type=F32)
        part[dz] = both.astype(BF16).reshape(2, 2, ctx, 256)
        keys = kv[dz].reshape(group, 256)[:, 0:128]
        dqt[...] += lax.dot_general(keys, y[:, 0:pair], TN, preferred_element_type=F32)

    sib = {}
    from_yl = {}
    from_peer = []

    def to_sibling(dz):
        sib[dz] = net.start(part.at[dz, 1], sib_in.at[dz], p.sibling())

    def chip_sum(t, dz):
        return part[dz, 0, t].astype(F32) + sib_in[dz, t].astype(F32)

    def to_y(dz):
        sib[dz].wait_recv()
        yl_out[dz] = chip_sum(1, dz).astype(BF16)
        from_yl[dz] = net.start(yl_out.at[dz], yl_in.at[dz], p.other_yl())

    def both_sum(dz):
        from_yl[dz].wait_recv()
        return chip_sum(0, dz) + yl_in[dz].astype(F32)

    def to_peer(dz):
        value = both_sum(dz)
        z_sums[dz] = value.astype(BF16)
        block = z_sums.at[dz]
        if dz == 4:
            stepped["half", 6] = net.start(block.at[upper], half_in.at[0], p.along_z(-2))
            stepped["half", 2] = net.start(block.at[lower], half_in.at[1], p.along_z(2))
        elif dz == 5:
            stepped["whole", 6] = net.start(block, step_in.at[0], p.along_z(-1))
        elif dz == 3:
            stepped["whole", 2] = net.start(block, step_in.at[1], p.along_z(1))
        elif dz in (7, 1):
            ended.append(net.start(block, end_in.at[len(ended)], p.along_z(1 if dz == 1 else -1)))

    def to_owner(dz):
        side, rows_of = (0, upper) if dz == 6 else (1, lower)
        value = both_sum(dz)
        stepped["whole", dz].wait_recv()
        z_sums[dz] = (value + step_in[side].astype(F32)).astype(BF16)
        stepped["half", dz].wait_recv()
        z_sums[dz, rows_of] = (z_sums[dz, rows_of].astype(F32) + half_in[side].astype(F32)).astype(BF16)
        ended.append(net.start(z_sums.at[dz], end_in.at[len(ended)], p.along_z(2 if dz == 2 else -2)))

    stepped = {}
    ended = []
    order = (4, 5, 3, 6, 2, 7, 1, 0)
    for i, dz in enumerate(order):
        grads(dz)
        to_sibling(dz)
        if i >= 2:
            to_y(order[i - 2])
        if i >= 5:
            to_peer(order[i - 5])

    to_y(1)
    to_owner(6)
    to_y(0)
    to_owner(2)
    turned = jnp.concatenate([dqt[0:HEAD_DIM, 0:rows], dqt[HEAD_DIM:128, rows:pair]], axis=0) * scale
    dq = turned.T.astype(BF16)
    turned = turned.astype(BF16)
    dq_full[h] = dq
    dq_y = net.start(dq_full.at[h], dq_full.at[h], p.across(0))
    dq_x = [net.start(dq_full.at[h], dq_full.at[h], p.along_x(d)) for d in (2, 1, 3)]
    to_peer(7)
    to_peer(1)

    for copy in vol_x:
        copy.wait_recv()
    for i in range(4):
        block = jnp.concatenate([vol_full[2 * i], vol_full[2 * i + 1]], axis=1)
        q_part[i // 2, i % 2] = jnp.dot(turned, block, preferred_element_type=F32).astype(BF16)
    q_sib = net.start(q_part.at[1 - p.c], q_core, p.sibling())

    own = both_sum(0)
    for i, copy in enumerate(ended):
        copy.wait_recv()
        own = own + end_in[i].astype(F32)
    dkv_quad[0] = own.astype(BF16)
    dkv_copies = [net.start(dkv_quad.at[0], dkv_quad.at[3 - i], square[i]) for i in range(3)]
    dq_y.wait_recv()
    dq_x += [net.start(dq_full.at[hp], dq_full.at[hp], p.along_x(d)) for d in (2, 1, 3)]
    q_sib.wait_recv()
    q_yl[...] = (q_part[p.c].astype(F32) + q_core[...].astype(F32)).astype(BF16)
    q_copy = net.start(q_yl.at[1 - p.yl], q_yl_in, p.other_yl())
    dkv = dkv_quad[0]
    for i in range(NX):
        weights = jnp.concatenate([w_key[i * 256 : i * 256 + 256, :], w_value[i * 256 : i * 256 + 256, :]], axis=1)
        surf_out[i] = lax.dot_general(dkv, weights, NT, preferred_element_type=F32).astype(BF16)
    surf_x = [net.start(surf_out.at[(p.x + d) % NX], surf_in.at[d - 1], p.along_x(d)) for d in (2, 1, 3)]
    q_copy.wait_recv()
    z_out[:, :, 256:384] = (q_yl[p.yl].astype(F32) + q_yl_in[...].astype(F32)).T.reshape(NZ, 32, 128).astype(BF16)

    for copy in squares + dkv_copies:
        copy.wait_recv()
    dkv = dkv_quad[...].reshape(4 * ctx, 256)
    for i in range(2):
        points = jnp.concatenate([surf_quad[j, i] for j in range(4)], axis=0)
        block = lax.dot_general(points, dkv, TN, preferred_element_type=F32).astype(BF16)
        z_out[i * 4 : i * 4 + 4, :, 0:256] = block.reshape(4, 32, 256)

    far_first = (4, 3, 5, 2, 6, 1, 7)
    scattered = [net.start(z_out.at[(p.z + d) % NZ], z_in.at[d - 1], p.along_z(d)) for d in far_first]
    for copy in scattered:
        copy.wait_recv()
    sums = z_out[p.z].astype(F32)
    for i in range(NZ - 1):
        sums = sums + z_in[i].astype(F32)
    out[quarter, p.z] = sums.astype(BF16)

    def forward(dz):
        block = out.at[quarter, (p.z + dz) % NZ]
        return net.start(block, block, p.other_yl())

    mine = out.at[quarter, p.z]
    gathered = {d: net.start(mine, mine, p.along_z(d)) for d in far_first}
    forwarded = [forward(0)]

    def sum_x(copies, out, arrived, mid):
        for copy in copies:
            copy.wait_recv()
        sums = out[p.x].astype(F32)
        for i in range(NX - 1):
            sums = sums + arrived[i].astype(F32)
        mid[0] = sums[:, 0:128].astype(BF16)
        mid[1] = sums[:, 128:256].astype(BF16)

    sum_x(surf_x, surf_out, surf_in, surf_mid)
    surf_copy = net.start(surf_mid.at[1 - p.yh], surf_end, p.across(0))
    near_first = (1, 7, 2, 6, 3, 5, 4)
    for dz in near_first:
        gathered[NZ - dz].wait_recv()
        forwarded.append(forward(dz))
    to_core = [net.start(out.at[quarter], out.at[quarter], p.sibling())]
    hold(out.at[quarter], w_result.at[quarter])
    for copy in dq_x + swapped:
        copy.wait_recv()
    every = jnp.concatenate([dq_full[i] for i in range(8)], axis=1)
    weights = jnp.concatenate([w_rows[i] for i in range(8)], axis=1)
    grad_vol[...] = lax.dot_general(every, weights, NT, preferred_element_type=F32).astype(BF16)
    hold(grad_vol, vol_result)
    for copy, dz in zip(forwarded, (0,) + near_first):
        copy.wait_recv()
        block = out.at[p.c * 2 + 1 - p.yl, (p.z + dz) % NZ]
        to_core.append(net.start(block, block, p.sibling()))
    theirs = p.c * 2 + 1 - p.yl
    hold(out.at[theirs], w_result.at[theirs])
    surf_copy.wait_recv()
    grad_surf[...] = (surf_mid[p.yh].astype(F32) + surf_end[...].astype(F32)).astype(BF16)
    hold(grad_surf, surf_result)
    for copy in to_core:
        copy.wait_recv()
    side = pl.ds((1 - p.c) * 2, 2)
    hold(out.at[side], w_result.at[side])
    for copy in held[6:]:
        copy.wait()
    net.finish()


def finish_kernel(vol_in, surf_in, w_in, grad_vol, grad_surf, grad_wq, grad_wk, grad_wv):
    grad_vol[...] = vol_in[...]
    grad_surf[...] = surf_in[...]
    grad_wk[...] = w_in[:, 0:128].astype(F32)
    grad_wv[...] = w_in[:, 128:256].astype(F32)
    grad_wq[...] = w_in[:, 256:384].astype(F32)


def in_vmem(count):
    return [pl.BlockSpec(memory_space=pltpu.VMEM)] * count


def struct(*shape):
    return jax.ShapeDtypeStruct(shape, BF16)


def on_device(vol, surf, w_query, w_key, w_value, grad_out):
    rows, ctx = vol.shape[0], surf.shape[0]
    pair = 2 * rows
    group = 4 * ctx

    def over_x(n):
        return [
            pltpu.VMEM((NX, n, 256), BF16), pltpu.VMEM((NX - 1, n, 256), BF16),
            pltpu.VMEM((2, n, 128), BF16), pltpu.VMEM((n, 128), BF16),
        ]

    grad_vol, grad_surf, out = pl.pallas_call(
        whole_kernel,
        out_shape=[struct(rows, 128), struct(ctx, 128), struct(4, NZ, 32, 384)],
        in_specs=[pl.BlockSpec(memory_space=pl.ANY)] * 6,
        out_specs=[pl.BlockSpec(memory_space=pl.ANY)] * 3,
        scratch_shapes=[
            pltpu.VMEM((1024, 128), BF16),
            pltpu.VMEM((1024, 128), BF16),
            pltpu.VMEM((1024, 128), BF16),
            pltpu.VMEM((rows, 128), BF16),
            pltpu.VMEM((rows, 128), BF16),
            pltpu.VMEM((ctx, 128), BF16),
            pltpu.VMEM((4, NZ, 32, 384), BF16),
            pltpu.SemaphoreType.DMA((12,)),
            pltpu.VMEM((NZ, 2, 2, ctx, 256), BF16),
            pltpu.VMEM((8, rows, 128), BF16),
            pltpu.VMEM((8, ctx, 128), BF16),
            pltpu.VMEM((512, 128), BF16),
            pltpu.VMEM((rows, 128), BF16),
            pltpu.VMEM((rows, 128), BF16),
            pltpu.VMEM((4, 2, ctx, 128), BF16),
            pltpu.VMEM((4, ctx, 256), BF16),
            pltpu.VMEM((NZ * group, 2 * pair), F32),
            pltpu.VMEM((group, 2 * pair), BF16),
            pltpu.VMEM((2 * pair, 256), BF16),
            pltpu.VMEM((256, 2 * pair), BF16),
            pltpu.VMEM((128, pair), F32),
            pltpu.VMEM((8, pair), F32),
            pltpu.VMEM((8, pair), F32),
            pltpu.VMEM((8, pair), F32),
            pltpu.VMEM((NZ, 2, 2, ctx, 256), BF16),
            pltpu.VMEM((NZ, 2, ctx, 256), BF16),
            pltpu.VMEM((NZ, ctx, 256), BF16),
            pltpu.VMEM((NZ, ctx, 256), BF16),
            pltpu.VMEM((NZ, ctx, 256), BF16),
            pltpu.VMEM((2, ctx, 256), BF16),
            pltpu.VMEM((2, ctx // 2, 256), BF16),
            pltpu.VMEM((4, ctx, 256), BF16),
        ]
        + [pltpu.VMEM((8, 128, 128), BF16), pltpu.VMEM((8, rows, 128), BF16)]
        + over_x(ctx)
        + [
            pltpu.VMEM((2, 2, 128, 256), BF16),
            pltpu.VMEM((2, 128, 256), BF16),
            pltpu.VMEM((2, 128, 256), BF16),
            pltpu.VMEM((128, 256), BF16),
            pltpu.VMEM((NZ, 32, 384), BF16),
            pltpu.VMEM((NZ - 1, 32, 384), BF16),
        ]
        + [pltpu.SemaphoreType.DMA((130,)), pltpu.SemaphoreType.DMA((130,))],
        compiler_params=pltpu.CompilerParams(collective_id=0, has_side_effects=True, vmem_limit_bytes=VMEM_LIMIT),
    )(vol, surf, w_query, w_key, w_value, grad_out)

    wide = jax.ShapeDtypeStruct((1024, 128), F32)
    return pl.pallas_call(
        finish_kernel,
        out_shape=[struct(rows, 128), struct(ctx, 128), wide, wide, wide],
        in_specs=in_vmem(3),
        out_specs=in_vmem(5),
    )(grad_vol, grad_surf, out.reshape(1024, 384))


def solution(mesh):
    in_specs = (
        P("blk", "heads"),
        P("blk", "heads"),
        P(None, "heads"),
        P(None, "heads"),
        P(None, "heads"),
        P("blk", "heads"),
    )
    out_specs = (
        P("blk", "heads"),
        P("blk", "heads"),
        P(None, "heads"),
        P(None, "heads"),
        P(None, "heads"),
    )
    return jax.shard_map(
        on_device, mesh=mesh, in_specs=in_specs, out_specs=out_specs, check_vma=False
    )
```

```python
import jax
import jax.numpy as jnp
from jax import lax
from jax.experimental import pallas as pl
from jax.experimental.pallas import tpu as pltpu
from jax.sharding import PartitionSpec as P

HEAD_DIM = 64
MESH = pl.DeviceIdType.MESH
VMEM_LIMIT = 60 * 1024 * 1024
F32 = jnp.float32
BF16 = jnp.bfloat16
NT = (((1,), (1,)), ((), ()))
TN = (((0,), (0,)), ((), ()))

NX, NZ = 4, 8


class Place:
    def __init__(self):
        self.h = lax.axis_index("heads")
        self.b = lax.axis_index("blk")
        self.x, self.yh = self.h // 2, self.h % 2
        self.yl, self.z, self.c = self.b // 16, (self.b // 2) % NZ, self.b % 2

    def along_x(self, d):
        return (((self.x + d) % NX) * 2 + self.yh, self.b)

    def across(self, d):
        return (((self.x + d) % NX) * 2 + 1 - self.yh, self.b)

    def along_z(self, d):
        return (self.h, self.yl * 16 + ((self.z + d) % NZ) * 2 + self.c)

    def other_yl(self):
        return (self.h, (1 - self.yl) * 16 + self.z * 2 + self.c)

    def sibling(self):
        return (self.h, self.yl * 16 + self.z * 2 + 1 - self.c)

    def diagonal(self):
        return (self.h, (1 - self.yl) * 16 + self.z * 2 + 1 - self.c)


def meet(partners):
    barrier = pltpu.get_barrier_semaphore()
    for partner in partners:
        pl.semaphore_signal(barrier, inc=1, device_id=partner, device_id_type=MESH)
    pl.semaphore_wait(barrier, len(partners))


class Sender:
    def __init__(self, send_sem, recv_sem):
        self.send_sem, self.recv_sem = send_sem, recv_sem
        self.used = 0
        self.all = []

    def start(self, src, dst, device):
        copy = pltpu.make_async_remote_copy(
            src_ref=src,
            dst_ref=dst,
            send_sem=self.send_sem.at[self.used],
            recv_sem=self.recv_sem.at[self.used],
            device_id=device,
            device_id_type=MESH,
        )
        self.used += 1
        copy.start()
        self.all.append(copy)
        return copy

    def finish(self):
        for copy in self.all:
            copy.wait_send()


def whole_kernel(
    vol, surf, w_query_in, w_key_in, w_value_in, grad_in,
    vol_result, surf_result, w_result,
    w_query, w_key, w_value, grad_out, grad_vol, grad_surf, out, local_sem,
    kv, vol_full, surf_full, w_far, query_out, query_in, surf_quad, dkv_quad, x, y, m, mt, dqt, top, total, weighted,
    part, sib_in, yl_out, yl_in, z_sums, step_in, half_in, end_in, near_out, near_in,
    vol_out, vol_in, vol_mid, vol_end, surf_out, surf_in, surf_mid, surf_end,
    q_part, q_core, q_yl, q_yl_in, z_out, z_in,
    send_sem, recv_sem,
):
    p = Place()
    h = p.h
    hp = p.x * 2 + 1 - p.yh
    rows, ctx = vol.shape[0], surf.shape[0]
    group = 4 * ctx
    pair = 2 * rows
    tiles = pair // 128
    scale = HEAD_DIM**-0.5
    heads = [p.across(d) for d in (2, 1, 3)] + [p.along_x(2), p.across(0), p.along_x(1), p.along_x(3)]
    square = [p.diagonal(), p.other_yl(), p.sibling()]
    held = []

    def hold(src, dst):
        held.append(pltpu.make_async_copy(src, dst, local_sem.at[len(held)]))
        held[-1].start()

    hold(grad_in, grad_out)
    hold(surf, surf_full.at[h])
    hold(w_key_in, w_key)
    hold(w_value_in, w_value)
    hold(vol, vol_full.at[h])
    hold(w_query_in, w_query)
    meet(heads + square + [p.along_z(d) for d in range(1, NZ)])
    net = Sender(send_sem, recv_sem)

    surf_all = [net.start(surf, surf_full.at[h], peer) for peer in heads]
    vol_x = [net.start(vol, vol_full.at[h], p.along_x(d)) for d in (2, 1, 3)]
    far = []
    for i in range(NX):
        rows_far = pl.ds(pl.multiple_of((i * 2 + 1 - p.yh) * 128, 128), 128)
        far.append(net.start(w_query_in.at[rows_far], w_far.at[pl.ds(i * 128, 128)], p.across(0)))

    def place(index, block):
        turned = block.T
        col = lax.broadcasted_iota(jnp.int32, block.shape, 1)
        row = lax.broadcasted_iota(jnp.int32, turned.shape, 0)
        for head in (0, 1):
            at = index * pair + head * rows
            m[at : at + rows, index * 128 : index * 128 + 128] = jnp.where(col // HEAD_DIM == head, block, 0.0).astype(BF16)
            mt[index * 128 : index * 128 + 128, at : at + rows] = jnp.where(row // HEAD_DIM == head, turned, 0.0).astype(BF16)

    m[...] = jnp.zeros_like(m)
    mt[...] = jnp.zeros_like(mt)
    for copy in held:
        copy.wait()
    place(1, grad_out[...].astype(F32))
    top[...] = jnp.full_like(top, -jnp.inf)
    total[...] = jnp.zeros_like(total)
    weighted[...] = jnp.zeros_like(weighted)

    for copy in surf_all:
        copy.wait_recv()
    features = jnp.concatenate([surf_full[i] for i in range(8)], axis=1)
    kv[0, 0, 0, :, 0:128] = jnp.dot(features, w_key[...], preferred_element_type=F32).astype(BF16)
    kv[0, 0, 0, :, 128:256] = jnp.dot(features, w_value[...], preferred_element_type=F32).astype(BF16)

    arrivals = {}
    over_y = {}
    shared = {}
    mid = ctx // 2
    upper, lower = slice(0, mid), slice(mid, ctx)

    def share(dz):
        shared[dz] = net.start(kv.at[dz, 0], kv.at[dz, 1], p.sibling())

    def along(dz, d):
        to = (dz - d) % NZ
        arrivals[to] = [net.start(kv.at[dz, 0, 0], kv.at[to, 0, 0], p.along_z(d))]

    def hand_on(dz):
        over_y[dz] = net.start(kv.at[dz, 0, 0], kv.at[dz, 0, 1], p.other_yl())

    def from_z(*groups):
        for dz in groups:
            for copy in arrivals[dz]:
                copy.wait_recv()
            if dz == 6:
                along(6, 1)
                from_below = net.start(kv.at[6, 0, 0, upper], kv.at[4, 0, 0, upper], p.along_z(2))
            if dz == 2:
                along(2, -1)
                from_above = net.start(kv.at[2, 0, 0, lower], kv.at[4, 0, 0, lower], p.along_z(-2))
                arrivals[4] = [from_below, from_above]
            if dz not in (7, 1):
                hand_on(dz)

    def from_y(*groups):
        for dz in groups:
            over_y[dz].wait_recv()
            if dz == 0:
                for d in (1, -1):
                    over_y[-d % NZ] = net.start(kv.at[0, 0, 1], kv.at[-d % NZ, 0, 1], p.along_z(d))
            share(dz)

    for d in (2, -2, 1, -1):
        along(0, d)
    hand_on(0)
    from_y(0)

    for copy in vol_x + far:
        copy.wait_recv()
    features = jnp.concatenate([vol_full[i * 2 + p.yh] for i in range(NX)], axis=1)
    query_out[...] = jnp.dot(features, w_far[...], preferred_element_type=F32).astype(BF16)
    query_copy = net.start(query_out, query_in, p.across(0))
    from_z(6, 2)
    from_z(7, 1)
    near = [w_query[pl.ds(pl.multiple_of((i * 2 + p.yh) * 128, 128), 128), :] for i in range(NX)]
    query = jnp.dot(features, jnp.concatenate(near, axis=0), preferred_element_type=F32)
    from_y(6, 2)
    from_z(5, 3)
    from_z(4)
    from_y(7, 1)
    vol_y = net.start(vol, vol_full.at[h], p.across(0))
    query_copy.wait_recv()
    query = (query + query_in[...].astype(F32)).astype(BF16)
    place(0, query.astype(F32) * scale)

    def scan(dz):
        at = pl.ds(pl.multiple_of(dz * group, group), group)
        x[at, :] = jnp.dot(kv[dz].reshape(group, 256), mt[...], preferred_element_type=F32)
        for j in range(tiles):
            cols = slice(j * 128, j * 128 + 128)
            scores = x[at, cols].reshape(group // 8, 8, 128)
            dprob = x[at, pair + j * 128 : pair + j * 128 + 128].reshape(group // 8, 8, 128)
            before = top[:, cols]
            now = jnp.maximum(before, jnp.max(scores, axis=0))
            expo = jnp.exp(scores - now[None])
            fade = jnp.exp(before - now)
            top[:, cols] = now
            total[:, cols] = total[:, cols] * fade + jnp.sum(expo, axis=0)
            weighted[:, cols] = weighted[:, cols] * fade + jnp.sum(expo * dprob, axis=0)

    def have(*groups):
        for dz in groups:
            shared[dz].wait_recv()

    have(0)
    scan(0)
    have(6)
    scan(6)
    from_y(5, 3)
    have(2)
    scan(2)
    from_y(4)
    quarter = p.c * 2 + p.yl
    surf_quad[0] = surf_full[pl.ds(quarter * 2, 2)]
    squares = []
    for slot, device, its in (
        (3, p.diagonal(), (1 - p.c) * 2 + 1 - p.yl),
        (2, p.other_yl(), p.c * 2 + 1 - p.yl),
        (1, p.sibling(), (1 - p.c) * 2 + p.yl),
    ):
        squares.append(net.start(surf_full.at[pl.ds(its * 2, 2)], surf_quad.at[slot], device))
    have(7, 1)
    scan(7)
    scan(1)
    have(5, 3)
    scan(5)
    scan(3)
    vol_y.wait_recv()
    vol_x = [net.start(vol_full.at[hp], vol_full.at[hp], p.along_x(d)) for d in (2, 1, 3)]
    have(4)
    scan(4)

    best = jnp.max(top[...], axis=0, keepdims=True)
    fade = jnp.exp(top[...] - best)
    sums = jnp.sum(total[...] * fade, axis=0, keepdims=True)
    delta = jnp.sum(weighted[...] * fade, axis=0, keepdims=True) / sums
    top[...] = jnp.broadcast_to(best, top.shape)
    total[...] = jnp.broadcast_to(jnp.log(sums), total.shape)
    weighted[...] = jnp.broadcast_to(delta, weighted.shape)
    dqt[...] = jnp.zeros_like(dqt)

    def grads(dz):
        at = pl.ds(pl.multiple_of(dz * group, group), group)
        for j in range(tiles):
            cols = slice(j * 128, j * 128 + 128)
            more = slice(pair + j * 128, pair + j * 128 + 128)
            scores = x[at, cols].reshape(group // 8, 8, 128)
            dprob = x[at, more].reshape(group // 8, 8, 128)
            probs = jnp.exp((scores - top[:, cols][None]) - total[:, cols][None])
            dscore = probs * (dprob - weighted[:, cols][None])
            y[:, cols] = dscore.reshape(group, 128).astype(BF16)
            y[:, more] = probs.reshape(group, 128).astype(BF16)
        both = jnp.dot(y[...], m[...], preferred_element_type=F32)
        part[dz] = both.astype(BF16).reshape(2, 2, ctx, 256)
        keys = kv[dz].reshape(group, 256)[:, 0:128]
        dqt[...] += lax.dot_general(keys, y[:, 0:pair], TN, preferred_element_type=F32)

    sib = {}
    from_yl = {}
    from_peer = []

    def to_sibling(dz):
        sib[dz] = net.start(part.at[dz, 1], sib_in.at[dz], p.sibling())

    def chip_sum(t, dz):
        return part[dz, 0, t].astype(F32) + sib_in[dz, t].astype(F32)

    def to_y(dz):
        sib[dz].wait_recv()
        yl_out[dz] = chip_sum(1, dz).astype(BF16)
        from_yl[dz] = net.start(yl_out.at[dz], yl_in.at[dz], p.other_yl())

    def to_near(dz):
        side = 0 if dz == 7 else 1
        sib[dz].wait_recv()
        for t in (0, 1):
            near_out[side, t] = chip_sum(t, dz).astype(BF16)
        nears.append(net.start(near_out.at[side], near_in.at[side], p.along_z(2 * side - 1)))

    def both_sum(dz):
        from_yl[dz].wait_recv()
        return chip_sum(0, dz) + yl_in[dz].astype(F32)

    def to_peer(dz):
        value = both_sum(dz)
        z_sums[dz] = value.astype(BF16)
        block = z_sums.at[dz]
        if dz == 4:
            stepped["half", 6] = net.start(block.at[upper], half_in.at[0], p.along_z(-2))
            stepped["half", 2] = net.start(block.at[lower], half_in.at[1], p.along_z(2))
        elif dz == 5:
            stepped["whole", 6] = net.start(block, step_in.at[0], p.along_z(-1))
        elif dz == 3:
            stepped["whole", 2] = net.start(block, step_in.at[1], p.along_z(1))

    def to_owner(dz):
        side, rows_of = (0, upper) if dz == 6 else (1, lower)
        value = both_sum(dz)
        stepped["whole", dz].wait_recv()
        z_sums[dz] = (value + step_in[side].astype(F32)).astype(BF16)
        stepped["half", dz].wait_recv()
        z_sums[dz, rows_of] = (z_sums[dz, rows_of].astype(F32) + half_in[side].astype(F32)).astype(BF16)
        ended.append(net.start(z_sums.at[dz], end_in.at[len(ended)], p.along_z(2 if dz == 2 else -2)))

    stepped = {}
    ended = []
    nears = []
    order = (4, 5, 3, 6, 2, 7, 1, 0)
    for i, dz in enumerate(order):
        grads(dz)
        to_sibling(dz)
        if i >= 2:
            (to_near if order[i - 2] in (7, 1) else to_y)(order[i - 2])
        if i >= 5:
            to_peer(order[i - 5])

    to_near(1)
    to_owner(6)
    to_owner(2)
    turned = jnp.concatenate([dqt[0:HEAD_DIM, 0:rows], dqt[HEAD_DIM:128, rows:pair]], axis=0) * scale
    dq = turned.T.astype(BF16)
    turned = turned.astype(BF16)
    for copy in nears:
        copy.wait_recv()
    sib[0].wait_recv()
    both = chip_sum(1, 0) + near_in[0, 1].astype(F32) + near_in[1, 1].astype(F32)
    yl_out[0] = both.astype(BF16)
    from_yl[0] = net.start(yl_out.at[0], yl_in.at[0], p.other_yl())

    for i in range(NX):
        vol_out[i] = lax.dot_general(dq, w_query[i * 256 : i * 256 + 256, :], NT, preferred_element_type=F32).astype(BF16)
    for copy in vol_x:
        copy.wait_recv()
    vol_x = [net.start(vol_out.at[(p.x + d) % NX], vol_in.at[d - 1], p.along_x(d)) for d in (2, 1, 3)]
    for i in range(4):
        block = jnp.concatenate([vol_full[2 * i], vol_full[2 * i + 1]], axis=1)
        q_part[i // 2, i % 2] = jnp.dot(turned, block, preferred_element_type=F32).astype(BF16)
    q_sib = net.start(q_part.at[1 - p.c], q_core, p.sibling())

    own = both_sum(0) + near_in[0, 0].astype(F32) + near_in[1, 0].astype(F32)
    for i, copy in enumerate(ended):
        copy.wait_recv()
        own = own + end_in[i].astype(F32)
    dkv_quad[0] = own.astype(BF16)
    dkv_copies = [net.start(dkv_quad.at[0], dkv_quad.at[3 - i], square[i]) for i in range(3)]
    q_sib.wait_recv()
    q_yl[...] = (q_part[p.c].astype(F32) + q_core[...].astype(F32)).astype(BF16)
    q_copy = net.start(q_yl.at[1 - p.yl], q_yl_in, p.other_yl())
    dkv = dkv_quad[0]
    for i in range(NX):
        weights = jnp.concatenate([w_key[i * 256 : i * 256 + 256, :], w_value[i * 256 : i * 256 + 256, :]], axis=1)
        surf_out[i] = lax.dot_general(dkv, weights, NT, preferred_element_type=F32).astype(BF16)
    surf_x = [net.start(surf_out.at[(p.x + d) % NX], surf_in.at[d - 1], p.along_x(d)) for d in (2, 1, 3)]
    q_copy.wait_recv()
    z_out[:, :, 256:384] = (q_yl[p.yl].astype(F32) + q_yl_in[...].astype(F32)).T.reshape(NZ, 32, 128).astype(BF16)

    for copy in squares + dkv_copies:
        copy.wait_recv()
    dkv = dkv_quad[...].reshape(4 * ctx, 256)
    for i in range(2):
        points = jnp.concatenate([surf_quad[j, i] for j in range(4)], axis=0)
        block = lax.dot_general(points, dkv, TN, preferred_element_type=F32).astype(BF16)
        z_out[i * 4 : i * 4 + 4, :, 0:256] = block.reshape(4, 32, 256)

    far_first = (4, 3, 5, 2, 6, 1, 7)
    scattered = [net.start(z_out.at[(p.z + d) % NZ], z_in.at[d - 1], p.along_z(d)) for d in far_first]
    for copy in scattered:
        copy.wait_recv()
    sums = z_out[p.z].astype(F32)
    for i in range(NZ - 1):
        sums = sums + z_in[i].astype(F32)
    out[quarter, p.z] = sums.astype(BF16)

    def forward(dz):
        block = out.at[quarter, (p.z + dz) % NZ]
        return net.start(block, block, p.other_yl())

    mine = out.at[quarter, p.z]
    gathered = {d: net.start(mine, mine, p.along_z(d)) for d in far_first}
    forwarded = [forward(0)]

    def sum_x(copies, out, arrived, mid):
        for copy in copies:
            copy.wait_recv()
        sums = out[p.x].astype(F32)
        for i in range(NX - 1):
            sums = sums + arrived[i].astype(F32)
        mid[0] = sums[:, 0:128].astype(BF16)
        mid[1] = sums[:, 128:256].astype(BF16)

    sum_x(surf_x, surf_out, surf_in, surf_mid)
    surf_copy = net.start(surf_mid.at[1 - p.yh], surf_end, p.across(0))
    near_first = (1, 7, 2, 6, 3, 5, 4)
    for dz in near_first[0:4]:
        gathered[NZ - dz].wait_recv()
        forwarded.append(forward(dz))
    sum_x(vol_x, vol_out, vol_in, vol_mid)
    vol_copy = net.start(vol_mid.at[1 - p.yh], vol_end, p.across(0))
    for dz in near_first[4:]:
        gathered[NZ - dz].wait_recv()
        forwarded.append(forward(dz))
    to_core = [net.start(out.at[quarter], out.at[quarter], p.sibling())]
    hold(out.at[quarter], w_result.at[quarter])
    for copy, dz in zip(forwarded, (0,) + near_first):
        copy.wait_recv()
        block = out.at[p.c * 2 + 1 - p.yl, (p.z + dz) % NZ]
        to_core.append(net.start(block, block, p.sibling()))
    theirs = p.c * 2 + 1 - p.yl
    hold(out.at[theirs], w_result.at[theirs])
    surf_copy.wait_recv()
    grad_surf[...] = (surf_mid[p.yh].astype(F32) + surf_end[...].astype(F32)).astype(BF16)
    vol_copy.wait_recv()
    grad_vol[...] = (vol_mid[p.yh].astype(F32) + vol_end[...].astype(F32)).astype(BF16)
    hold(grad_vol, vol_result)
    hold(grad_surf, surf_result)
    for copy in to_core:
        copy.wait_recv()
    side = pl.ds((1 - p.c) * 2, 2)
    hold(out.at[side], w_result.at[side])
    for copy in held[6:]:
        copy.wait()
    net.finish()


def finish_kernel(vol_in, surf_in, w_in, grad_vol, grad_surf, grad_wq, grad_wk, grad_wv):
    grad_vol[...] = vol_in[...]
    grad_surf[...] = surf_in[...]
    grad_wk[...] = w_in[:, 0:128].astype(F32)
    grad_wv[...] = w_in[:, 128:256].astype(F32)
    grad_wq[...] = w_in[:, 256:384].astype(F32)


def in_vmem(count):
    return [pl.BlockSpec(memory_space=pltpu.VMEM)] * count


def struct(*shape):
    return jax.ShapeDtypeStruct(shape, BF16)


def on_device(vol, surf, w_query, w_key, w_value, grad_out):
    rows, ctx = vol.shape[0], surf.shape[0]
    pair = 2 * rows
    group = 4 * ctx

    def over_x(n):
        return [
            pltpu.VMEM((NX, n, 256), BF16), pltpu.VMEM((NX - 1, n, 256), BF16),
            pltpu.VMEM((2, n, 128), BF16), pltpu.VMEM((n, 128), BF16),
        ]

    grad_vol, grad_surf, out = pl.pallas_call(
        whole_kernel,
        out_shape=[struct(rows, 128), struct(ctx, 128), struct(4, NZ, 32, 384)],
        in_specs=[pl.BlockSpec(memory_space=pl.ANY)] * 6,
        out_specs=[pl.BlockSpec(memory_space=pl.ANY)] * 3,
        scratch_shapes=[
            pltpu.VMEM((1024, 128), BF16),
            pltpu.VMEM((1024, 128), BF16),
            pltpu.VMEM((1024, 128), BF16),
            pltpu.VMEM((rows, 128), BF16),
            pltpu.VMEM((rows, 128), BF16),
            pltpu.VMEM((ctx, 128), BF16),
            pltpu.VMEM((4, NZ, 32, 384), BF16),
            pltpu.SemaphoreType.DMA((12,)),
            pltpu.VMEM((NZ, 2, 2, ctx, 256), BF16),
            pltpu.VMEM((8, rows, 128), BF16),
            pltpu.VMEM((8, ctx, 128), BF16),
            pltpu.VMEM((512, 128), BF16),
            pltpu.VMEM((rows, 128), BF16),
            pltpu.VMEM((rows, 128), BF16),
            pltpu.VMEM((4, 2, ctx, 128), BF16),
            pltpu.VMEM((4, ctx, 256), BF16),
            pltpu.VMEM((NZ * group, 2 * pair), F32),
            pltpu.VMEM((group, 2 * pair), BF16),
            pltpu.VMEM((2 * pair, 256), BF16),
            pltpu.VMEM((256, 2 * pair), BF16),
            pltpu.VMEM((128, pair), F32),
            pltpu.VMEM((8, pair), F32),
            pltpu.VMEM((8, pair), F32),
            pltpu.VMEM((8, pair), F32),
            pltpu.VMEM((NZ, 2, 2, ctx, 256), BF16),
            pltpu.VMEM((NZ, 2, ctx, 256), BF16),
            pltpu.VMEM((NZ, ctx, 256), BF16),
            pltpu.VMEM((NZ, ctx, 256), BF16),
            pltpu.VMEM((NZ, ctx, 256), BF16),
            pltpu.VMEM((2, ctx, 256), BF16),
            pltpu.VMEM((2, ctx // 2, 256), BF16),
            pltpu.VMEM((2, ctx, 256), BF16),
            pltpu.VMEM((2, 2, ctx, 256), BF16),
            pltpu.VMEM((2, 2, ctx, 256), BF16),
        ]
        + over_x(rows) + over_x(ctx)
        + [
            pltpu.VMEM((2, 2, 128, 256), BF16),
            pltpu.VMEM((2, 128, 256), BF16),
            pltpu.VMEM((2, 128, 256), BF16),
            pltpu.VMEM((128, 256), BF16),
            pltpu.VMEM((NZ, 32, 384), BF16),
            pltpu.VMEM((NZ - 1, 32, 384), BF16),
        ]
        + [pltpu.SemaphoreType.DMA((130,)), pltpu.SemaphoreType.DMA((130,))],
        compiler_params=pltpu.CompilerParams(collective_id=0, has_side_effects=True, vmem_limit_bytes=VMEM_LIMIT),
    )(vol, surf, w_query, w_key, w_value, grad_out)

    wide = jax.ShapeDtypeStruct((1024, 128), F32)
    return pl.pallas_call(
        finish_kernel,
        out_shape=[struct(rows, 128), struct(ctx, 128), wide, wide, wide],
        in_specs=in_vmem(3),
        out_specs=in_vmem(5),
    )(grad_vol, grad_surf, out.reshape(1024, 384))


def solution(mesh):
    in_specs = (
        P("blk", "heads"),
        P("blk", "heads"),
        P(None, "heads"),
        P(None, "heads"),
        P(None, "heads"),
        P("blk", "heads"),
    )
    out_specs = (
        P("blk", "heads"),
        P("blk", "heads"),
        P(None, "heads"),
        P(None, "heads"),
        P(None, "heads"),
    )
    return jax.shard_map(
        on_device, mesh=mesh, in_specs=in_specs, out_specs=out_specs, check_vma=False
    )
```
